512 devices in a mesh: dp: 64 (over x_hi, z, core), mp: 8 (over x_lo, y).
Axes of the slice: x: 4 (x_hi: 2, x_lo: 2; x = x_hi * 2 + x_lo), y: 4, z: 16, core: 2. Of those that a mesh axis runs over, the one named last changes fastest.
Arguments:
- picture_tower_outputs: bfloat16 [8192, 1408], P('dp', 'mp'), may hold values from -200 to 200
- caption_tower_outputs: bfloat16 [8192, 1408], P('dp', 'mp'), may hold values from -200 to 200
- picture_mapping_matrix: bfloat16 [1408, 1536], P('mp'), may hold values from -1 to 1
- caption_mapping_matrix: bfloat16 [1408, 1536], P('mp'), may hold values from -1 to 1
- sharpness_factor: float32 [1], replicated, may hold values from 15 to 25
- offset_vector: float32 [1], replicated, may hold values from -10 to -6
Outputs:
- loss: float32 [1], replicated
- image_grad: float32 [8192, 1536], P('dp', 'mp')
- text_grad: float32 [8192, 1536], P(('dp', 'mp'))
The draws below stay inside these ranges and needn't reach their ends.
All inputs are finite; a program needn't handle non-finite values.
Results may differ from the reference program's by a relative error of at most 0.0084.
Values may be sent and summed in bfloat16 or wider, within the bound.
No kernel may reach another device: no remote copies, remote signals or barrier semaphores. Data moves between devices by JAX's collectives and lax.ppermute only.
A program may use at most 64 MiB of HBM per device.

```python
import jax
import jax.numpy as jnp
from jax import lax

W = 1408
E = 1536
TOK_DEV = 128
TOKENS = 8192
N_DP = 64


def shared_rows(key):
    group_key, vector_key, pair_key = jax.random.split(key, 3)
    groups = TOKENS // 4
    member_entry = jax.random.randint(group_key, (TOKENS,), 0, groups)
    centers = jax.random.truncated_normal(vector_key, -4.0, 4.0, (groups, W), jnp.float32)
    paired = jax.random.truncated_normal(pair_key, -4.0, 4.0, (TOKENS, W), jnp.float32)
    common_part = jax.random.truncated_normal(jax.random.fold_in(key, 99), -4.0, 4.0, (W,), jnp.float32)
    return (centers[member_entry], paired, common_part)


def feature_rows(shared, own_key, spread_top):
    class_part, pair_part, common_part = shared
    noise_key, scale_key = jax.random.split(own_key)
    own_noise = jax.random.truncated_normal(noise_key, -4.0, 4.0, (TOKENS, W), jnp.float32)
    position = jnp.arange(TOKENS, dtype=jnp.float32) / TOKENS
    noise_weight = 0.35 + 0.9 * position
    row_scale = jnp.exp(jax.random.uniform(scale_key, (TOKENS, 1), jnp.float32, 0.0, jnp.log(spread_top)))
    blended = 0.6 * class_part + 0.6 * pair_part + noise_weight[:, None] * own_noise
    return row_scale * blended


def draw_picture_tower_outputs(key, part):
    shared = shared_rows(key)
    key = jax.random.fold_in(key, 11)
    values = feature_rows(shared, key, 10.0)
    return values.astype(jnp.bfloat16)


def draw_caption_tower_outputs(key, part):
    shared = shared_rows(key)
    key = jax.random.fold_in(key, 12)
    values = feature_rows(shared, key, 10.0)
    return values.astype(jnp.bfloat16)


def shared_weight(key):
    return jax.random.truncated_normal(jax.random.fold_in(key, 7), -4.0, 4.0, (W, E), jnp.float32)


def projection(common_part, own_key, column_top):
    noise_key, column_key = jax.random.split(own_key, 2)
    normal_part = jax.random.truncated_normal(noise_key, -4.0, 4.0, (W, E), jnp.float32)
    own_noise = normal_part
    half_log = 0.5 * jnp.log(column_top)
    column_scale = jnp.exp(jax.random.uniform(column_key, (1, E), jnp.float32, -half_log, half_log))
    return column_scale * (0.8 * common_part + 0.6 * own_noise) / jnp.sqrt(jnp.float32(W * E))


def draw_picture_mapping_matrix(key, part):
    common_part = shared_weight(key)
    key = jax.random.fold_in(key, 21)
    values = projection(common_part, key, 10.0)
    return values.astype(jnp.bfloat16)


def draw_caption_mapping_matrix(key, part):
    common_part = shared_weight(key)
    key = jax.random.fold_in(key, 22)
    values = projection(common_part, key, 10.0)
    return values.astype(jnp.bfloat16)


def setup_inputs(seed: int = 0) -> dict:
    streams_of = jax.random.split(jax.random.key(seed), 7)
    picture_tower_outputs = draw_picture_tower_outputs(jax.random.fold_in(streams_of[6], 71), 0)
    caption_tower_outputs = draw_caption_tower_outputs(jax.random.fold_in(streams_of[6], 71), 0)
    picture_mapping_matrix = draw_picture_mapping_matrix(jax.random.fold_in(streams_of[6], 71), 0)
    caption_mapping_matrix = draw_caption_mapping_matrix(jax.random.fold_in(streams_of[6], 71), 0)
    sharpness_factor = jnp.clip(jax.random.uniform(streams_of[4], (1,), jnp.float32, 15.0, 25.0), 15.0, 25.0)
    offset_vector = jnp.clip(jax.random.uniform(streams_of[5], (1,), jnp.float32, -10.0, -6.0), -10.0, -6.0)
    return {"picture_tower_outputs": picture_tower_outputs, "caption_tower_outputs": caption_tower_outputs, "picture_mapping_matrix": picture_mapping_matrix, "caption_mapping_matrix": caption_mapping_matrix, "sharpness_factor": sharpness_factor, "offset_vector": offset_vector}


EPSILON = 1e-06

def normalize(embedded):
    inverse = lax.rsqrt(lax.optimization_barrier(jnp.sum(embedded * embedded, axis=1, keepdims=True)) + EPSILON)
    return (inverse, (embedded * inverse).astype(jnp.bfloat16))

def tangent_back(embedded, inverse, cotangent):
    row_dot = lax.optimization_barrier(jnp.sum(embedded * cotangent, axis=1, keepdims=True))
    return inverse * cotangent - inverse * inverse * inverse * embedded * row_dot

def reference(picture_tower_outputs, caption_tower_outputs, picture_mapping_matrix, caption_mapping_matrix, sharpness_factor, offset_vector):
    u_img = jnp.dot(picture_tower_outputs, picture_mapping_matrix, preferred_element_type=jnp.float32)
    u_txt = jnp.dot(caption_tower_outputs, caption_mapping_matrix, preferred_element_type=jnp.float32)
    inv_img, picture_unit_vectors = normalize(u_img)
    inv_txt, caption_unit_vectors = normalize(u_txt)
    affinity_multiplier = sharpness_factor[0]
    affinity_offset = offset_vector[0]
    pair_count = caption_unit_vectors.shape[0]
    blocks = picture_unit_vectors.reshape(N_DP, TOK_DEV, E)
    text_ids = jnp.arange(pair_count, dtype=jnp.int32)

    def visit_block(carried, scan_item):
        caption_derivative, loss_sum = carried
        picture_tile, block_idx = scan_item
        similarity_values = lax.dot_general(picture_tile, caption_unit_vectors, (((1,), (1,)), ((), ())), preferred_element_type=jnp.float32)
        affinity_matrix = affinity_multiplier * similarity_values + affinity_offset
        image_ids = block_idx * TOK_DEV + jnp.arange(TOK_DEV, dtype=jnp.int32)
        labels = jnp.where(image_ids[:, None] == text_ids[None, :], 1.0, -1.0).astype(jnp.float32)
        margin = labels * affinity_matrix
        loss_sum = loss_sum + jnp.sum(jax.nn.softplus(-margin))
        coefficient = (-labels * jax.nn.sigmoid(-margin)).astype(jnp.bfloat16)
        picture_derivative = affinity_multiplier * jnp.dot(coefficient, caption_unit_vectors, preferred_element_type=jnp.float32)
        caption_derivative = caption_derivative + affinity_multiplier * lax.dot_general(coefficient, picture_tile, (((0,), (0,)), ((), ())), preferred_element_type=jnp.float32)
        return ((caption_derivative, loss_sum), picture_derivative)
    start_state = (jnp.zeros((pair_count, E), jnp.float32), jnp.zeros((), jnp.float32))
    (caption_derivative, loss_sum), picture_derivative = lax.scan(visit_block, start_state, (blocks, jnp.arange(N_DP, dtype=jnp.int32)))
    image_grad = tangent_back(u_img, inv_img, picture_derivative.reshape(pair_count, E))
    text_grad = tangent_back(u_txt, inv_txt, caption_derivative)
    loss = (loss_sum / pair_count).reshape(1)
    return (loss, image_grad, text_grad)
```

```python
import jax
import jax.numpy as jnp
from jax import lax
from jax.sharding import Mesh, PartitionSpec as P

EPSILON = 1e-06
BF = jnp.bfloat16
F32 = jnp.float32

PARTS = (2, 16, 2, 2, 4)
NAMES = ("xh", "z", "core", "xl", "y")
DP = ("xh", "z", "core")
MP = ("xl", "y")
XY = ("xh", "xl", "y")
N_MP = 8
N_XY = 16
N_Z = 16
PAIRS = 8192


def exchange(value, axes):
    return lax.all_to_all(value, axes, 0, 0, tiled=True)


def other_core(value):
    return lax.ppermute(value, "core", [(0, 1), (1, 0)])


def split_pair(value):
    high = lax.reduce_precision(value, 8, 7)
    return high.astype(BF), (value - high).astype(BF)


def couple(images, texts, scale, offset, same):
    similarity = lax.dot_general(
        images, texts, (((1,), (1,)), ((), ())), preferred_element_type=F32
    )
    labels = jnp.where(same, 1.0, -1.0).astype(F32)
    margin = labels * (scale * similarity + offset)
    loss = jnp.sum(jax.nn.softplus(-margin))
    weight = (-labels * jax.nn.sigmoid(-margin)).astype(BF)
    return loss, weight


def on_device(x_img, x_txt, w_img, w_txt, sharpness_factor, offset_vector):
    scale = sharpness_factor[0]
    offset = offset_vector[0]
    rows = x_img.shape[0]
    shard = rows // N_MP
    width = w_img.shape[1]
    columns = width // N_MP
    xh, z_at = lax.axis_index("xh"), lax.axis_index("z")
    at_xy = lax.axis_index(XY)

    part_img = jnp.dot(x_img, w_img, preferred_element_type=F32).astype(BF)
    part_txt = jnp.dot(x_txt, w_txt, preferred_element_type=F32).astype(BF)
    parts = jnp.concatenate(
        [part_img.reshape(N_MP, shard, width), part_txt.reshape(N_MP, shard, width)], axis=1
    )
    parts = exchange(parts, MP)
    u = jnp.sum(parts.astype(F32), axis=0)
    inverse = lax.rsqrt(jnp.sum(u * u, axis=1, keepdims=True) + EPSILON)
    unit = (u * inverse).astype(BF)
    u_txt, inv_txt = u[shard:], inverse[shard:]
    unit_txt = unit[shard:]
    high, low = split_pair(inverse[:shard])
    unit_img = jnp.concatenate(
        [unit[:shard], high, low, jnp.zeros((shard, 126), BF)], axis=1
    )

    texts = exchange(jnp.broadcast_to(unit_txt, (N_Z,) + unit_txt.shape), ("z",))
    texts = texts.reshape(N_Z * shard, width)
    mine = exchange(jnp.broadcast_to(unit_img, (N_XY,) + unit_img.shape), XY)
    mine = mine.reshape(N_XY * shard, width + 128)
    inv_mine = mine[:, width].astype(F32) + mine[:, width + 1].astype(F32)
    mine = mine[:, :width]
    theirs = other_core(mine)

    image_ids = jnp.arange(N_XY * shard, dtype=jnp.int32)
    text_ids = jnp.arange(N_Z * shard, dtype=jnp.int32)
    same = (
        (image_ids[:, None] // shard == at_xy)
        & (text_ids[None, :] // shard == z_at)
        & (image_ids[:, None] % shard == text_ids[None, :] % shard)
    )
    loss_a, weight_a = couple(mine, texts, scale, offset, same)
    loss_b, weight_b = couple(theirs, texts, scale, offset, jnp.zeros_like(same))
    loss = lax.psum((loss_a + loss_b).reshape(1, 1), "core")

    back = (((0,), (0,)), ((), ()))
    grad_txt = scale * (
        lax.dot_general(weight_a, mine, back, preferred_element_type=F32)
        + lax.dot_general(weight_b, theirs, back, preferred_element_type=F32)
    )
    grad_txt = grad_txt.astype(BF).reshape(N_Z, shard, width)
    high, low = split_pair(loss)
    tag = jnp.concatenate([high, low, jnp.zeros((1, 126), BF)], axis=1)
    tag = jnp.broadcast_to(tag[None], (N_Z, shard, 128))
    sums = exchange(jnp.concatenate([grad_txt, tag], axis=2), ("z",))
    sums = jnp.sum(sums.astype(F32), axis=0)
    loss = sums[0:1, width : width + 1] + sums[0:1, width + 1 : width + 2]
    grad_txt = sums[:, :width]
    row_dot = jnp.sum(u_txt * grad_txt, axis=1, keepdims=True)
    text_grad = inv_txt * grad_txt - inv_txt * inv_txt * inv_txt * u_txt * row_dot

    def tangent(images, weight):
        grad = jnp.dot(weight, texts, preferred_element_type=F32)
        images = images.astype(F32)
        return grad - images * jnp.sum(images * grad, axis=1, keepdims=True)

    from_other = other_core(tangent(theirs, weight_b).astype(BF))
    term = tangent(mine, weight_a) + from_other.astype(F32)
    term = (scale * inv_mine[:, None]) * term
    term = term.astype(BF).reshape(2, rows, N_MP, columns).transpose(0, 2, 1, 3)
    term = term.reshape(N_XY, rows, columns)
    high, low = split_pair(loss)
    tag = jnp.concatenate([high, low, jnp.zeros((1, 62), BF)], axis=1)
    tag = jnp.broadcast_to(tag[None], (N_XY, rows, 64))
    sums = exchange(jnp.concatenate([term, tag], axis=2), XY)
    sums = jnp.sum(sums.astype(F32), axis=0)
    image_grad = sums[:, :columns]
    loss = (sums[0, columns] + sums[0, columns + 1]) / PAIRS
    return loss.reshape(1), image_grad, text_grad


def solution(mesh):
    parts = Mesh(mesh.devices.reshape(PARTS), NAMES)
    return jax.shard_map(
        on_device,
        mesh=parts,
        in_specs=(P(DP, MP), P(DP, MP), P(MP, None), P(MP, None), P(), P()),
        out_specs=(P(), P(DP, MP), P(DP + MP, None)),
        check_vma=False,
    )
```

```python
import jax
import jax.numpy as jnp
from jax import lax
from jax.sharding import Mesh, PartitionSpec as P

EPSILON = 1e-06
BF = jnp.bfloat16
F32 = jnp.float32

PARTS = (2, 8, 2, 2, 2, 4)
NAMES = ("xh", "zh", "zl", "core", "xl", "y")
DP = ("xh", "zh", "zl", "core")
Z = ("zh", "zl")
MP = ("xl", "y")
XY = ("xh", "xl", "y")
N_MP = 8
N_XY = 16
N_Z = 16
N_ZH = 8
PAIRS = 8192


def exchange(value, axes):
    return lax.all_to_all(value, axes, 0, 0, tiled=True)


def other_core(value):
    return lax.ppermute(value, "core", [(0, 1), (1, 0)])


def along_z(value, step):
    return lax.ppermute(value, Z, [(i, (i + step) % N_Z) for i in range(N_Z)])


def split_pair(value):
    high = lax.reduce_precision(value, 8, 7)
    return high.astype(BF), (value - high).astype(BF)


def couple(images, texts, scale, offset, same):
    similarity = lax.dot_general(
        images, texts, (((1,), (1,)), ((), ())), preferred_element_type=F32
    )
    labels = jnp.where(same, 1.0, -1.0).astype(F32)
    margin = labels * (scale * similarity + offset)
    loss = jnp.sum(jax.nn.softplus(-margin))
    weight = (-labels * jax.nn.sigmoid(-margin)).astype(BF)
    return loss, weight


def on_device(x_img, x_txt, w_img, w_txt, sharpness_factor, offset_vector):
    scale = sharpness_factor[0]
    offset = offset_vector[0]
    rows = x_img.shape[0]
    shard = rows // N_MP
    width = w_img.shape[1]
    columns = width // N_MP
    zh = lax.axis_index("zh")
    at_xy = lax.axis_index(XY)

    part_img = jnp.dot(x_img, w_img, preferred_element_type=F32).astype(BF)
    part_txt = jnp.dot(x_txt, w_txt, preferred_element_type=F32).astype(BF)
    parts = jnp.concatenate(
        [part_img.reshape(N_MP, shard, width), part_txt.reshape(N_MP, shard, width)], axis=1
    )
    parts = exchange(parts, MP)
    u = jnp.sum(parts.astype(F32), axis=0)
    inverse = lax.rsqrt(jnp.sum(u * u, axis=1, keepdims=True) + EPSILON)
    unit = (u * inverse).astype(BF)
    u_txt, inv_txt = u[shard:], inverse[shard:]
    unit_txt = unit[shard:]
    high, low = split_pair(inverse[:shard])
    unit_img = jnp.concatenate(
        [unit[:shard], high, low, jnp.zeros((shard, 126), BF)], axis=1
    )

    even = exchange(jnp.broadcast_to(unit_txt, (N_ZH,) + unit_txt.shape), ("zh",))
    mine = lax.all_gather(unit_img, XY, axis=0, tiled=True)
    even = even.reshape(N_ZH * shard, width)
    half = N_ZH * shard // 2
    odd = jnp.concatenate([along_z(even[:half], -1), along_z(even[half:], 1)], axis=0)
    inv_mine = mine[:, width].astype(F32) + mine[:, width + 1].astype(F32)
    mine = mine[:, :width]
    theirs = other_core(mine)
    texts = jnp.concatenate([even, odd], axis=0)

    image_ids = jnp.arange(N_XY * shard, dtype=jnp.int32)
    text_ids = jnp.arange(2 * N_ZH * shard, dtype=jnp.int32)
    same = (
        (image_ids[:, None] // shard == at_xy)
        & (text_ids[None, :] // shard == zh)
        & (image_ids[:, None] % shard == text_ids[None, :] % shard)
    )
    loss_a, weight_a = couple(mine, texts, scale, offset, same)
    loss_b, weight_b = couple(theirs, texts, scale, offset, jnp.zeros_like(same))
    loss = (loss_a + loss_b).reshape(1, 1)
    loss = loss + other_core(loss)
    loss = loss + lax.ppermute(loss, "zl", [(0, 1), (1, 0)])

    back = (((0,), (0,)), ((), ()))
    grad_txt = scale * (
        lax.dot_general(weight_a, mine, back, preferred_element_type=F32)
        + lax.dot_general(weight_b, theirs, back, preferred_element_type=F32)
    )
    grad_odd = grad_txt[2 * half :].astype(BF)
    from_up = along_z(grad_odd[:half], -1)
    from_down = along_z(grad_odd[half:], 1)

    def tangent(images, weight):
        grad = jnp.dot(weight, texts, preferred_element_type=F32)
        images = images.astype(F32)
        return grad - images * jnp.sum(images * grad, axis=1, keepdims=True)

    from_other = other_core(tangent(theirs, weight_b).astype(BF))
    term = tangent(mine, weight_a) + from_other.astype(F32)
    term = (scale * inv_mine[:, None]) * term
    term = term.astype(BF).reshape(2, rows, N_MP, columns).transpose(0, 2, 1, 3)
    term = term.reshape(N_XY, rows, columns)
    high, low = split_pair(loss)
    tag = jnp.concatenate([high, low, jnp.zeros((1, 62), BF)], axis=1)
    tag = jnp.broadcast_to(tag[None], (N_XY, rows, 64))
    sums = exchange(jnp.concatenate([term, tag], axis=2), XY)
    sums = jnp.sum(sums.astype(F32), axis=0)
    image_grad = sums[:, :columns]
    loss = (sums[0, columns] + sums[0, columns + 1]).reshape(1, 1)

    added = jnp.concatenate([from_up, from_down], axis=0).astype(F32)
    grad_txt = (grad_txt[: 2 * half] + added).astype(BF).reshape(N_ZH, shard, width)
    high, low = split_pair(loss)
    tag = jnp.concatenate([high, low, jnp.zeros((1, 126), BF)], axis=1)
    tag = jnp.broadcast_to(tag[None], (N_ZH, shard, 128))
    sums = exchange(jnp.concatenate([grad_txt, tag], axis=2), ("zh",))
    sums = jnp.sum(sums.astype(F32), axis=0)
    loss = (sums[0, width] + sums[0, width + 1]) / PAIRS
    grad_txt = sums[:, :width]
    row_dot = jnp.sum(u_txt * grad_txt, axis=1, keepdims=True)
    text_grad = inv_txt * grad_txt - inv_txt * inv_txt * inv_txt * u_txt * row_dot
    return loss.reshape(1), image_grad, text_grad


def solution(mesh):
    parts = Mesh(mesh.devices.reshape(PARTS), NAMES)
    return jax.shard_map(
        on_device,
        mesh=parts,
        in_specs=(P(DP, MP), P(DP, MP), P(MP, None), P(MP, None), P(), P()),
        out_specs=(P(), P(DP, MP), P(DP + MP, None)),
        check_vma=False,
    )
```

```python
import jax
import jax.numpy as jnp
from jax import lax
from jax.experimental import pallas as pl
from jax.experimental.pallas import tpu as pltpu
from jax.sharding import Mesh, PartitionSpec as P

EPSILON = 1e-06
BF = jnp.bfloat16
F32 = jnp.float32

PARTS = (2, 8, 2, 2, 2, 4)
NAMES = ("xh", "zh", "zl", "core", "xl", "y")
DP = ("xh", "zh", "zl", "core")
MP = ("xl", "y")
Z = ("zh", "zl")
XY = ("xh", "xl", "y")
N_MP = 8
N_XY = 16
N_Z = 16
N_ZH = 8
PAIRS = 8192
SHARD = 16
WIDTH = 1536
COLUMNS = WIDTH // N_MP
HALF = N_ZH * SHARD
IMAGES = N_XY * SHARD
LANES = 128
WIDE = WIDTH + LANES

VMEM = pl.BlockSpec(memory_space=pltpu.VMEM)
SMEM = pl.BlockSpec(memory_space=pltpu.SMEM)


def exchange(value, axes):
    return lax.all_to_all(value, axes, 0, 0, tiled=True)


def other_core(value):
    return lax.ppermute(value, "core", [(0, 1), (1, 0)])


def along_z(value, step):
    return lax.ppermute(value, Z, [(i, (i + step) % N_Z) for i in range(N_Z)])


def split_pair(value):
    high = lax.reduce_precision(value, 8, 7)
    return high.astype(BF), (value - high).astype(BF)


def call(body, outs, operands, specs, name, flops=0, moved=0, scratch=()):
    return pl.pallas_call(
        body,
        out_shape=[jax.ShapeDtypeStruct(shape, dtype) for shape, dtype in outs],
        in_specs=specs,
        out_specs=[VMEM] * len(outs),
        scratch_shapes=list(scratch),
        compiler_params=pltpu.CompilerParams(vmem_limit_bytes=24 * 1024 * 1024),
        cost_estimate=pl.CostEstimate(flops=flops, bytes_accessed=moved, transcendentals=0),
        name=name,
    )(*operands)


def dot(a, b, contract):
    return lax.dot_general(a, b, (contract, ((), ())), preferred_element_type=F32)


def terms(similarity, scale, offset, labels):
    value = -labels * (scale * similarity + offset)
    small = jnp.exp(-jnp.abs(value))
    loss = jnp.maximum(value, 0.0) + jnp.log1p(small)
    share = 1.0 / (1.0 + small)
    sigmoid = jnp.where(value >= 0.0, share, small * share)
    return loss, (-labels * sigmoid).astype(BF)


def tangent(images_ref, weight, texts, scale, row):
    rows = pl.ds(row, 128)
    grad = dot(weight, texts, ((1,), (0,)))
    images = images_ref[rows, :WIDTH].astype(F32)
    radial = jnp.sum(images * grad, axis=1, keepdims=True)
    tags = images_ref[rows, WIDTH:].astype(F32)
    inverse = tags[:, 0:1] + tags[:, 1:2]
    return (grad - images * radial) * (scale * inverse)


def pair_body(
    factors, place, mine_ref, theirs_ref, texts_ref,
    sent_ref, odd_ref, loss_ref, weight_ref,
):
    scale, offset = factors[0], factors[1]
    at_xy, at_z, parity = place[0], place[1], place[2]
    own = texts_ref[parity]
    other = texts_ref[1 - parity]
    texts = jnp.concatenate([own, other], axis=0)
    total = jnp.zeros((1, 2 * HALF), F32)
    for block in range(IMAGES // 128):
        rows = pl.ds(block * 128, 128)
        similarity = dot(theirs_ref[rows, :WIDTH], texts, ((1,), (1,)))
        loss, weight = terms(similarity, scale, offset, -1.0)
        total = total + jnp.sum(loss, axis=0, keepdims=True)
        weight_ref[pl.ds(IMAGES + block * 128, 128), :] = weight
        term = tangent(theirs_ref, weight, texts, scale, block * 128)
        sent_ref[rows, :] = term.astype(BF)
    for block in range(IMAGES // 128):
        rows = pl.ds(block * 128, 128)
        similarity = dot(mine_ref[rows, :WIDTH], texts, ((1,), (1,)))
        image = lax.broadcasted_iota(jnp.int32, similarity.shape, 0) + block * 128
        text = lax.broadcasted_iota(jnp.int32, similarity.shape, 1)
        same = (image // SHARD == at_xy) & (image - SHARD * at_xy == text - SHARD * at_z)
        labels = jnp.where(same, 1.0, -1.0)
        loss, weight = terms(similarity, scale, offset, labels)
        total = total + jnp.sum(loss, axis=0, keepdims=True)
        weight_ref[rows, :] = weight
    loss_ref[...] = jnp.broadcast_to(jnp.sum(total, axis=1, keepdims=True), loss_ref.shape)
    for start in range(0, WIDTH, 512):
        cols = pl.ds(start, 512)
        odd = dot(weight_ref[:IMAGES, HALF:], mine_ref[:, cols], ((0,), (0,)))
        odd += dot(weight_ref[IMAGES:, HALF:], theirs_ref[:, cols], ((0,), (0,)))
        odd_ref[:, cols] = (scale * odd).astype(BF)


def own_body(factors, place, mine_ref, theirs_ref, texts_ref, weight_ref, mine_term_ref, even_ref):
    scale = factors[0]
    parity = place[2]
    own = texts_ref[parity]
    other = texts_ref[1 - parity]
    texts = jnp.concatenate([own, other], axis=0)
    for block in range(IMAGES // 128):
        rows = pl.ds(block * 128, 128)
        mine_term_ref[rows, :] = tangent(
            mine_ref, weight_ref[rows, :], texts, scale, block * 128
        )
    for start in range(0, WIDTH, 512):
        cols = pl.ds(start, 512)
        even = dot(weight_ref[:IMAGES, :HALF], mine_ref[:, cols], ((0,), (0,)))
        even += dot(weight_ref[IMAGES:, :HALF], theirs_ref[:, cols], ((0,), (0,)))
        even_ref[:, cols] = scale * even


def lay_out_body(loss_ref, mine_term_ref, other_ref, out_ref):
    loss = jnp.broadcast_to(loss_ref[0:1, 0:1], (128, 64))
    high = loss.astype(BF)
    low = (loss - high.astype(F32)).astype(BF)
    lane = lax.broadcasted_iota(jnp.int32, (128, 64), 1)
    tag = jnp.where(lane == 0, high.astype(F32), jnp.where(lane == 1, low.astype(F32), 0.0))
    for block in range(IMAGES // 128):
        rows = pl.ds(block * 128, 128)
        for part in range(N_MP):
            cols = slice(part * COLUMNS, (part + 1) * COLUMNS)
            term = mine_term_ref[rows, cols] + other_ref[rows, cols].astype(F32)
            out_ref[block * N_MP + part] = jnp.concatenate([term, tag], axis=1).astype(BF)


def add_odd_body(loss_ref, even_ref, up_ref, down_ref, out_ref):
    loss = jnp.broadcast_to(loss_ref[0:1, 0:1], (SHARD, LANES))
    high = loss.astype(BF)
    low = (loss - high.astype(F32)).astype(BF)
    lane = lax.broadcasted_iota(jnp.int32, (SHARD, LANES), 1)
    tag = jnp.where(lane == 0, high.astype(F32), jnp.where(lane == 1, low.astype(F32), 0.0))
    for block in range(N_ZH):
        rows = pl.ds(block * SHARD, SHARD)
        side = up_ref if block < N_ZH // 2 else down_ref
        from_rows = pl.ds((block % (N_ZH // 2)) * SHARD, SHARD)
        total = even_ref[rows, :] + side[from_rows, :].astype(F32)
        out_ref[block, :, :WIDTH] = total.astype(BF)
        out_ref[block, :, WIDTH:] = tag.astype(BF)


def text_body(sums_ref, u_ref, inverse_ref, grad_ref, loss_ref):
    total = sums_ref[0].astype(F32)
    for block in range(1, N_ZH):
        total = total + sums_ref[block].astype(F32)
    tags = total[0:1, WIDTH:]
    loss_ref[...] = jnp.broadcast_to((tags[:, 0:1] + tags[:, 1:2]) * (1.0 / PAIRS), loss_ref.shape)
    grad = total[:, :WIDTH]
    u = u_ref[...]
    inverse = inverse_ref[...]
    row_dot = jnp.sum(u * grad, axis=1, keepdims=True)
    grad_ref[...] = inverse * grad - inverse * inverse * inverse * u * row_dot


def on_device(x_img, x_txt, w_img, w_txt, sharpness_factor, offset_vector):
    rows = x_img.shape[0]
    zh, zl = lax.axis_index("zh"), lax.axis_index("zl")
    factors = jnp.concatenate([sharpness_factor, offset_vector])
    place = jnp.stack([lax.axis_index(XY), zh, zl]).astype(jnp.int32)

    part_img = jnp.dot(x_img, w_img, preferred_element_type=F32).astype(BF)
    part_txt = jnp.dot(x_txt, w_txt, preferred_element_type=F32).astype(BF)
    parts = jnp.concatenate(
        [part_img.reshape(N_MP, SHARD, WIDTH), part_txt.reshape(N_MP, SHARD, WIDTH)], axis=1
    )
    parts = exchange(parts, MP)
    u = jnp.sum(parts.astype(F32), axis=0)
    inverse = lax.rsqrt(jnp.sum(u * u, axis=1, keepdims=True) + EPSILON)
    unit = (u * inverse).astype(BF)
    u_txt, inv_txt = u[SHARD:], inverse[SHARD:]
    unit_txt = unit[SHARD:]
    high, low = split_pair(inverse[:SHARD])
    unit_img = jnp.concatenate(
        [unit[:SHARD], high, low, jnp.zeros((SHARD, LANES - 2), BF)], axis=1
    )

    texts = exchange(jnp.broadcast_to(unit_txt, (N_Z, SHARD, WIDTH)), ("zl", "zh"))
    texts = texts.reshape(2, HALF, WIDTH)
    mine = lax.all_gather(unit_img, XY, axis=0, tiled=True)
    theirs = other_core(mine)

    sent, odd, loss, weight = call(
        pair_body,
        [((IMAGES, WIDTH), BF), ((HALF, WIDTH), BF), ((8, LANES), F32),
         ((2 * IMAGES, 2 * HALF), BF)],
        (factors, place, mine, theirs, texts), [SMEM, SMEM, VMEM, VMEM, VMEM], "pairs",
        flops=900_000_000, moved=4_000_000,
    )
    from_other = other_core(sent)
    swap = [(0, 1), (1, 0)]
    cross = [(0, 3), (1, 2), (2, 1), (3, 0)]
    loss = (
        loss
        + other_core(loss)
        + (lax.ppermute(loss, "zl", swap) + lax.ppermute(loss, ("zl", "core"), cross))
    )
    from_up = along_z(odd[: HALF // 2], -1)
    from_down = along_z(odd[HALF // 2 :], 1)
    mine_term, even = call(
        own_body,
        [((IMAGES, WIDTH), F32), ((HALF, WIDTH), F32)],
        (factors, place, mine, theirs, texts, weight),
        [SMEM, SMEM, VMEM, VMEM, VMEM, VMEM], "own",
        flops=400_000_000, moved=4_000_000,
    )

    (term,) = call(
        lay_out_body, [((N_XY, rows, 256), BF)], (loss, mine_term, from_other),
        [VMEM] * 3, "lay_out", moved=3_000_000,
    )
    sums = exchange(term, XY)
    sums = jnp.sum(sums.astype(F32), axis=0)
    image_grad = sums[:, :COLUMNS]
    loss = jnp.broadcast_to(sums[0:1, COLUMNS : COLUMNS + 1] + sums[0:1, COLUMNS + 1 : COLUMNS + 2], (8, LANES))

    (term,) = call(
        add_odd_body, [((N_ZH, SHARD, WIDE), BF)], (loss, even, from_up, from_down),
        [VMEM] * 4, "add_odd", moved=2_000_000,
    )
    sums = exchange(term, ("zh",))
    text_grad, loss = call(
        text_body, [((SHARD, WIDTH), F32), ((1, LANES), F32)], (sums, u_txt, inv_txt),
        [VMEM] * 3, "text", moved=1_000_000,
    )
    return loss[0, 0:1], image_grad, text_grad


def solution(mesh):
    parts = Mesh(mesh.devices.reshape(PARTS), NAMES)
    return jax.shard_map(
        on_device,
        mesh=parts,
        in_specs=(P(DP, MP), P(DP, MP), P(MP, None), P(MP, None), P(), P()),
        out_specs=(P(), P(DP, MP), P(DP + MP, None)),
        check_vma=False,
    )
```

```python
import jax
import jax.numpy as jnp
from jax import lax
from jax.experimental import pallas as pl
from jax.experimental.pallas import tpu as pltpu
from jax.sharding import Mesh, PartitionSpec as P

EPSILON = 1e-06
BF = jnp.bfloat16
F32 = jnp.float32

PARTS = (2, 16, 2, 2, 4)
NAMES = ("xh", "z", "core", "xl", "y")
DP = ("xh", "z", "core")
MP = ("xl", "y")
X = ("xh", "xl")
PLANE = ("xh", "core", "xl", "y")
N_MP = 8
N_PLANE = 32
N_Z = 16
PAIRS = 8192
SHARD = 16
WIDTH = 1536
COLUMNS = WIDTH // N_MP
BLOCK = 128
IMAGES = N_PLANE * SHARD
TEXTS = N_Z * SHARD
LANES = 128
WIDE = WIDTH + LANES
HALF = BLOCK // 2
PIECE = BLOCK + HALF

VMEM = pl.BlockSpec(memory_space=pltpu.VMEM)
SMEM = pl.BlockSpec(memory_space=pltpu.SMEM)


def exchange(value, axes):
    return lax.all_to_all(value, axes, 0, 0, tiled=True)


def other_core(value):
    return lax.ppermute(value, "core", [(0, 1), (1, 0)])


def along_x(value, flip):
    return lax.ppermute(value, X, [(i, i ^ flip) for i in range(4)])


def along_y(value, step):
    return lax.ppermute(value, "y", [(i, (i + step) % 4) for i in range(4)])


def split_pair(value):
    high = lax.reduce_precision(value, 8, 7)
    return high.astype(BF), (value - high).astype(BF)


def call(body, outs, operands, specs, name, flops=0, moved=0):
    return pl.pallas_call(
        body,
        out_shape=[jax.ShapeDtypeStruct(shape, dtype) for shape, dtype in outs],
        in_specs=specs,
        out_specs=[VMEM] * len(outs),
        compiler_params=pltpu.CompilerParams(vmem_limit_bytes=24 * 1024 * 1024),
        cost_estimate=pl.CostEstimate(flops=flops, bytes_accessed=moved, transcendentals=0),
        name=name,
    )(*operands)


def dot(a, b, contract):
    return lax.dot_general(a, b, (contract, ((), ())), preferred_element_type=F32)


def terms(similarity, scale, offset, labels):
    value = -labels * (scale * similarity + offset)
    small = jnp.exp(-jnp.abs(value))
    loss = jnp.maximum(value, 0.0) + jnp.log1p(small)
    share = 1.0 / (1.0 + small)
    sigmoid = jnp.where(value >= 0.0, share, small * share)
    return loss, (-labels * sigmoid).astype(BF)


def weights_body(factors, place, images_ref, texts_ref, weight_ref, loss_ref):
    scale, offset = factors[0], factors[1]
    at_plane, at_z = place[0], place[1]
    total = jnp.zeros((1, TEXTS), F32)
    for block in range(IMAGES // BLOCK):
        rows = pl.ds(block * BLOCK, BLOCK)
        similarity = dot(images_ref[rows, :WIDTH], texts_ref[...], ((1,), (1,)))
        image = lax.broadcasted_iota(jnp.int32, similarity.shape, 0) + block * BLOCK
        text = lax.broadcasted_iota(jnp.int32, similarity.shape, 1)
        same = (image // SHARD == at_plane) & (image - SHARD * at_plane == text - SHARD * at_z)
        loss, weight = terms(similarity, scale, offset, jnp.where(same, 1.0, -1.0))
        total = total + jnp.sum(loss, axis=0, keepdims=True)
        weight_ref[rows, :] = weight
    loss_ref[...] = jnp.broadcast_to(jnp.sum(total, axis=1, keepdims=True), loss_ref.shape)


def text_sums_body(factors, loss_ref, images_ref, weight_ref, out_ref):
    scale = factors[0]
    loss = jnp.broadcast_to(loss_ref[0:1, 0:1], (SHARD, LANES))
    high = loss.astype(BF)
    low = (loss - high.astype(F32)).astype(BF)
    lane = lax.broadcasted_iota(jnp.int32, (SHARD, LANES), 1)
    tag = jnp.where(lane == 0, high.astype(F32), jnp.where(lane == 1, low.astype(F32), 0.0))
    for start in range(0, WIDTH, 256):
        cols = pl.ds(start, 256)
        grad = scale * dot(weight_ref[...], images_ref[:, cols], ((0,), (0,)))
        for plane in range(N_Z):
            out_ref[plane, :, cols] = grad[plane * SHARD : (plane + 1) * SHARD].astype(BF)
    for plane in range(N_Z):
        out_ref[plane, :, WIDTH:] = tag.astype(BF)


def image_terms_body(factors, place, images_ref, texts_ref, weight_ref, kept_ref, sent_ref):
    scale = factors[0]
    core = place[2]
    for hi in range(2):
        for out_ref, side in ((sent_ref, 1 - core), (kept_ref, core)):
            rows = pl.ds(pl.multiple_of((hi * 2 + side) * BLOCK, BLOCK), BLOCK)
            grad = dot(weight_ref[rows, :], texts_ref[...], ((1,), (0,)))
            images = images_ref[rows, :WIDTH].astype(F32)
            radial = jnp.sum(images * grad, axis=1, keepdims=True)
            tags = images_ref[rows, WIDTH:].astype(F32)
            inverse = tags[:, 0:1] + tags[:, 1:2]
            term = (grad - images * radial) * (scale * inverse)
            for part in range(N_MP):
                at = part * COLUMNS
                piece = hi * N_MP + part
                out_ref[piece, :BLOCK] = term[:, at : at + BLOCK].astype(out_ref.dtype)
                rest = term[:, at + BLOCK : at + COLUMNS]
                rest = jnp.concatenate([rest[:HALF], rest[HALF:]], axis=1)
                out_ref[piece, BLOCK:] = rest.astype(out_ref.dtype)


def add_core_body(place, kept_ref, other_ref, own_ref, one_ref, two_ref, three_ref):
    at_x = place[3]
    for flip, out_ref in enumerate((own_ref, one_ref, two_ref, three_ref)):
        first = jnp.bitwise_xor(at_x, flip) * 4
        for y in range(4):
            total = kept_ref[first + y] + other_ref[first + y].astype(F32)
            out_ref[y] = total.astype(out_ref.dtype)


def add_x_body(place, own_ref, a_ref, b_ref, c_ref, mine_ref, one_ref, two_ref, three_ref):
    at_y = place[4]
    for step, out_ref in enumerate((mine_ref, one_ref, two_ref, three_ref)):
        y = lax.rem(at_y + step, 4)
        total = own_ref[y] + a_ref[y].astype(F32) + (b_ref[y].astype(F32) + c_ref[y].astype(F32))
        out_ref[...] = total.astype(out_ref.dtype)


def add_y_body(mine_ref, a_ref, b_ref, c_ref, grad_ref):
    total = mine_ref[...] + a_ref[...].astype(F32)
    total = total + (b_ref[...].astype(F32) + c_ref[...].astype(F32))
    grad_ref[:, :LANES] = total[:BLOCK]
    grad_ref[:HALF, LANES:] = total[BLOCK:, :HALF]
    grad_ref[HALF:, LANES:] = total[BLOCK:, HALF:]


def text_body(sums_ref, u_ref, inverse_ref, image_ref, grad_ref, loss_ref):
    total = sums_ref[0].astype(F32)
    for block in range(1, N_Z):
        total = total + sums_ref[block].astype(F32)
    tags = total[0:1, WIDTH:]
    loss_ref[...] = jnp.broadcast_to(tags[:, 0:1] + tags[:, 1:2], loss_ref.shape)
    grad = total[:, :WIDTH]
    u = u_ref[...]
    inverse = inverse_ref[...]
    row_dot = jnp.sum(u * grad, axis=1, keepdims=True)
    grad_ref[...] = inverse * grad - inverse * inverse * inverse * u * row_dot


def on_device(x_img, x_txt, w_img, w_txt, sharpness_factor, offset_vector):
    factors = jnp.concatenate([sharpness_factor, offset_vector])
    place = jnp.stack([lax.axis_index(axes) for axes in (PLANE, "z", "core", X, "y")])
    place = place.astype(jnp.int32)

    part_img = jnp.dot(x_img, w_img, preferred_element_type=F32).astype(BF)
    part_txt = jnp.dot(x_txt, w_txt, preferred_element_type=F32).astype(BF)
    parts = jnp.concatenate(
        [part_img.reshape(N_MP, SHARD, WIDTH), part_txt.reshape(N_MP, SHARD, WIDTH)], axis=1
    )
    parts = exchange(parts, MP)
    u = jnp.sum(parts.astype(F32), axis=0)
    inverse = lax.rsqrt(jnp.sum(u * u, axis=1, keepdims=True) + EPSILON)
    unit = (u * inverse).astype(BF)
    u_txt, inv_txt = u[SHARD:], inverse[SHARD:]
    unit_txt = unit[SHARD:]
    high, low = split_pair(inverse[:SHARD])
    unit_img = jnp.concatenate(
        [unit[:SHARD], high, low, jnp.zeros((SHARD, LANES - 2), BF)], axis=1
    )

    images = exchange(jnp.broadcast_to(unit_img, (N_PLANE, SHARD, WIDE)), PLANE)
    images = images.reshape(IMAGES, WIDE)
    texts = lax.all_gather(unit_txt, ("z",), axis=0, tiled=True)

    weight, loss = call(
        weights_body, [((IMAGES, TEXTS), BF), ((8, LANES), F32)],
        (factors, place, images, texts), [SMEM, SMEM, VMEM, VMEM], "weights",
        flops=403_000_000, moved=2_700_000,
    )

    (term,) = call(
        text_sums_body, [((N_Z, SHARD, WIDE), BF)], (factors, loss, images, weight),
        [SMEM, VMEM, VMEM, VMEM], "text_sums", flops=403_000_000, moved=2_700_000,
    )
    sums = exchange(term, ("z",))

    pieces = N_PLANE // 2
    kept, sent = call(
        image_terms_body, [((pieces, PIECE, LANES), F32), ((pieces, PIECE, LANES), BF)],
        (factors, place, images, texts, weight),
        [SMEM, SMEM, VMEM, VMEM, VMEM], "image_terms",
        flops=403_000_000, moved=4_700_000,
    )
    own, one, two, three = call(
        add_core_body, [((4, PIECE, LANES), F32)] + [((4, PIECE, LANES), BF)] * 3,
        (place, kept, other_core(sent)), [SMEM, VMEM, VMEM], "add_core", moved=3_000_000,
    )
    mine, one, two, three = call(
        add_x_body, [((PIECE, LANES), F32)] + [((PIECE, LANES), BF)] * 3,
        (place, own, along_x(one, 1), along_x(two, 2), along_x(three, 3)),
        [SMEM] + [VMEM] * 4, "add_x", moved=1_200_000,
    )
    (image_grad,) = call(
        add_y_body, [((BLOCK, COLUMNS), F32)],
        (mine, along_y(one, 1), along_y(two, 2), along_y(three, 3)),
        [VMEM] * 4, "add_y", moved=350_000,
    )

    text_grad, loss = call(
        text_body, [((SHARD, WIDTH), F32), ((8, LANES), F32)], (sums, u_txt, inv_txt, image_grad),
        [VMEM] * 3 + [pl.BlockSpec(memory_space=pl.ANY)], "text", moved=1_000_000,
    )
    loss = exchange(jnp.broadcast_to(loss, (N_PLANE, 8, LANES)), PLANE)
    loss = jnp.sum(loss, axis=0)[0, 0:1] * (1.0 / PAIRS)
    return loss, image_grad, text_grad


def solution(mesh):
    parts = Mesh(mesh.devices.reshape(PARTS), NAMES)
    return jax.shard_map(
        on_device,
        mesh=parts,
        in_specs=(P(DP, MP), P(DP, MP), P(MP, None), P(MP, None), P(), P()),
        out_specs=(P(), P(DP, MP), P(DP + MP, None)),
        check_vma=False,
    )
```

```python
import jax
import jax.numpy as jnp
from jax import lax
from jax.experimental import pallas as pl
from jax.experimental.pallas import tpu as pltpu
from jax.sharding import Mesh, PartitionSpec as P

EPSILON = 1e-06
BF = jnp.bfloat16
F32 = jnp.float32

PARTS = (2, 16, 2, 2, 4)
NAMES = ("xh", "z", "core", "xl", "y")
DP = ("xh", "z", "core")
MP = ("xl", "y")
X = ("xh", "xl")
PLANE = ("xh", "core", "xl", "y")
N_MP = 8
N_PLANE = 32
N_Z = 16
PAIRS = 8192
SHARD = 16
WIDTH = 1536
COLUMNS = WIDTH // N_MP
BLOCK = 128
IMAGES = N_PLANE * SHARD
TEXTS = N_Z * SHARD
LANES = 128
WIDE = WIDTH + LANES
HALF = BLOCK // 2
PIECE = BLOCK + HALF

CHUNK = 512
COPIED = 4
VMEM = pl.BlockSpec(memory_space=pltpu.VMEM)
HBM = pl.BlockSpec(memory_space=pltpu.HBM)


def exchange(value, axes):
    return lax.all_to_all(value, axes, 0, 0, tiled=True)


def other_core(value):
    return lax.ppermute(value, "core", [(0, 1), (1, 0)])


def along_x(value, flip):
    return lax.ppermute(value, X, [(i, i ^ flip) for i in range(4)])


def along_y(value, step):
    return lax.ppermute(value, "y", [(i, (i + step) % 4) for i in range(4)])


def call(body, outs, operands, specs, name, flops=0, moved=0):
    return pl.pallas_call(
        body,
        out_shape=[jax.ShapeDtypeStruct(shape, dtype) for shape, dtype in outs],
        in_specs=specs,
        out_specs=[VMEM] * len(outs),
        compiler_params=pltpu.CompilerParams(vmem_limit_bytes=24 * 1024 * 1024),
        cost_estimate=pl.CostEstimate(flops=flops, bytes_accessed=moved, transcendentals=0),
        name=name,
    )(*operands)


def dot(a, b, contract):
    return lax.dot_general(a, b, (contract, ((), ())), preferred_element_type=F32)


def terms(similarity, scale, offset, labels):
    value = -labels * (scale * similarity + offset)
    small = jnp.exp(-jnp.abs(value))
    loss = jnp.maximum(value, 0.0) + jnp.log1p(small)
    share = 1.0 / (1.0 + small)
    sigmoid = jnp.where(value >= 0.0, share, small * share)
    return loss, (-labels * sigmoid).astype(BF)


def loss_tag(total, rows):
    loss = jnp.broadcast_to(total, (rows, LANES))
    high = loss.astype(BF)
    low = (loss - high.astype(F32)).astype(BF)
    lane = lax.broadcasted_iota(jnp.int32, (rows, LANES), 1)
    tag = jnp.where(lane == 0, high.astype(F32), jnp.where(lane == 1, low.astype(F32), 0.0))
    return tag.astype(BF)


def normalize_body(parts_ref, images_hbm, text_ref, u_ref, inverse_ref, images_ref, sems):
    copies = []
    for at in (0, SHARD):
        rows = slice(at, at + SHARD)
        u = parts_ref[0, rows].astype(F32)
        for member in range(1, N_MP):
            u = u + parts_ref[member, rows].astype(F32)
        inverse = lax.rsqrt(jnp.sum(u * u, axis=1, keepdims=True) + EPSILON)
        unit = (u * inverse).astype(BF)
        if at:
            text_ref[...] = unit
            u_ref[...] = u
            inverse_ref[...] = jnp.broadcast_to(inverse, inverse_ref.shape)
        else:
            tag = loss_tag(inverse, SHARD)
            for piece in range(COPIED):
                images_ref[piece, :, :WIDTH] = unit
                images_ref[piece, :, WIDTH:] = tag
            for start in range(0, N_PLANE, COPIED):
                target = images_hbm.at[pl.ds(start, COPIED)]
                copies.append(pltpu.make_async_copy(images_ref, target, sems.at[start // COPIED]))
                copies[-1].start()
    for copy in copies:
        copy.wait()


def pairs_body(scale_ref, offset_ref, images_ref, texts_ref, weight_hbm, out_hbm, weight_ref, sums_ref, sems):
    scale, offset = scale_ref[...], offset_ref[...]
    at_plane, at_z = lax.axis_index(PLANE), lax.axis_index("z")
    copies = []

    def send(source, target):
        copies.append(pltpu.make_async_copy(source, target, sems.at[len(copies)]))
        copies[-1].start()

    total = jnp.zeros((1, TEXTS), F32)
    for block in range(IMAGES // BLOCK):
        rows = pl.ds(block * BLOCK, BLOCK)
        similarity = dot(images_ref[rows, :WIDTH], texts_ref[...], ((1,), (1,)))
        image = lax.broadcasted_iota(jnp.int32, similarity.shape, 0) + block * BLOCK
        text = lax.broadcasted_iota(jnp.int32, similarity.shape, 1)
        same = (image // SHARD == at_plane) & (image - SHARD * at_plane == text - SHARD * at_z)
        loss, weight = terms(similarity, scale, offset, jnp.where(same, 1.0, -1.0))
        total = total + jnp.sum(loss, axis=0, keepdims=True)
        weight_ref[rows, :] = weight
    send(weight_ref, weight_hbm)
    tag = loss_tag(jnp.sum(total, axis=1, keepdims=True), SHARD)
    for plane in range(N_Z):
        sums_ref[plane, :, WIDTH:] = tag
    for start in range(0, WIDTH, CHUNK):
        cols = pl.ds(start, CHUNK)
        grad = scale * dot(weight_ref[...], images_ref[:, cols], ((0,), (0,)))
        for plane in range(N_Z):
            sums_ref[plane, :, cols] = grad[plane * SHARD : (plane + 1) * SHARD].astype(BF)
        cols = pl.ds(start, CHUNK + (LANES if start + CHUNK == WIDTH else 0))
        send(sums_ref.at[:, :, cols], out_hbm.at[:, :, cols])
    for copy in copies:
        copy.wait()


def image_terms_body(scale_ref, images_ref, texts_ref, weight_ref, kept_ref, sent_ref):
    scale = scale_ref[...]
    core = lax.axis_index("core")
    for hi in range(2):
        for side_ref, side in ((sent_ref, 1 - core), (kept_ref, core)):
            rows = pl.ds(pl.multiple_of((hi * 2 + side) * BLOCK, BLOCK), BLOCK)
            grad = dot(weight_ref[rows, :], texts_ref[...], ((1,), (0,)))
            images = images_ref[rows, :WIDTH].astype(F32)
            radial = jnp.sum(images * grad, axis=1, keepdims=True)
            tags = images_ref[rows, WIDTH:].astype(F32)
            inverse = tags[:, 0:1] + tags[:, 1:2]
            term = (grad - images * radial) * (scale * inverse)
            for part in range(N_MP):
                at = part * COLUMNS
                piece = hi * N_MP + part
                side_ref[piece, :BLOCK] = term[:, at : at + BLOCK].astype(side_ref.dtype)
                rest = term[:, at + BLOCK : at + COLUMNS]
                rest = jnp.concatenate([rest[:HALF], rest[HALF:]], axis=1)
                side_ref[piece, BLOCK:] = rest.astype(side_ref.dtype)


def add_core_body(kept_ref, other_ref, own_ref, one_ref, two_ref, three_ref):
    at_x = lax.axis_index(X)
    for flip, out_ref in enumerate((own_ref, one_ref, two_ref, three_ref)):
        first = jnp.bitwise_xor(at_x, flip) * 4
        for y in range(4):
            total = kept_ref[first + y] + other_ref[first + y].astype(F32)
            out_ref[y] = total.astype(out_ref.dtype)


def add_x_body(own_ref, a_ref, b_ref, c_ref, mine_ref, one_ref, two_ref, three_ref):
    at_y = lax.axis_index("y")
    for step, out_ref in enumerate((mine_ref, one_ref, two_ref, three_ref)):
        y = lax.rem(at_y + step, 4)
        total = own_ref[y] + a_ref[y].astype(F32) + (b_ref[y].astype(F32) + c_ref[y].astype(F32))
        out_ref[...] = total.astype(out_ref.dtype)


def add_y_body(mine_ref, a_ref, b_ref, c_ref, grad_ref):
    total = mine_ref[...] + a_ref[...].astype(F32)
    total = total + (b_ref[...].astype(F32) + c_ref[...].astype(F32))
    grad_ref[:, :LANES] = total[:BLOCK]
    grad_ref[:HALF, LANES:] = total[BLOCK:, :HALF]
    grad_ref[HALF:, LANES:] = total[BLOCK:, HALF:]


def text_body(sums_ref, u_ref, inverse_ref, image_ref, grad_ref, loss_ref):
    total = sums_ref[0].astype(F32)
    for block in range(1, N_Z):
        total = total + sums_ref[block].astype(F32)
    tags = total[0:1, WIDTH:]
    loss_ref[...] = jnp.broadcast_to((tags[:, 0:1] + tags[:, 1:2])[None], loss_ref.shape)
    grad = total[:, :WIDTH]
    u = u_ref[...]
    inverse = inverse_ref[:, 0:1]
    row_dot = jnp.sum(u * grad, axis=1, keepdims=True)
    grad_ref[...] = inverse * grad - inverse * inverse * inverse * u * row_dot


def on_device(x_img, x_txt, w_img, w_txt, sharpness_factor, offset_vector):
    part_img = jnp.dot(x_img, w_img, preferred_element_type=F32).astype(BF)
    part_txt = jnp.dot(x_txt, w_txt, preferred_element_type=F32).astype(BF)
    parts = jnp.concatenate(
        [part_img.reshape(N_MP, SHARD, WIDTH), part_txt.reshape(N_MP, SHARD, WIDTH)], axis=1
    )
    parts = exchange(parts, MP)
    unit_img, unit_txt, u_txt, inv_txt = pl.pallas_call(
        normalize_body,
        out_shape=[
            pltpu.HBM((N_PLANE, SHARD, WIDE), BF),
            jax.ShapeDtypeStruct((SHARD, WIDTH), BF),
            jax.ShapeDtypeStruct((SHARD, WIDTH), F32),
            jax.ShapeDtypeStruct((SHARD, LANES), F32),
        ],
        in_specs=[VMEM],
        out_specs=[HBM, VMEM, VMEM, VMEM],
        scratch_shapes=[
            pltpu.VMEM((COPIED, SHARD, WIDE), BF),
            pltpu.SemaphoreType.DMA((N_PLANE // COPIED,)),
        ],
        compiler_params=pltpu.CompilerParams(vmem_limit_bytes=24 * 1024 * 1024),
        cost_estimate=pl.CostEstimate(flops=0, bytes_accessed=2_700_000, transcendentals=0),
        name="normalize",
    )(parts)

    images = exchange(unit_img, PLANE)
    images = images.reshape(IMAGES, WIDE)
    texts = lax.all_gather(unit_txt, ("z",), axis=0, tiled=True)

    scale, offset = sharpness_factor.reshape(1, 1), offset_vector.reshape(1, 1)
    weight, term = pl.pallas_call(
        pairs_body,
        out_shape=[pltpu.HBM((IMAGES, TEXTS), BF), pltpu.HBM((N_Z, SHARD, WIDE), BF)],
        in_specs=[VMEM] * 4,
        out_specs=[HBM, HBM],
        scratch_shapes=[
            pltpu.VMEM((IMAGES, TEXTS), BF),
            pltpu.VMEM((N_Z, SHARD, WIDE), BF),
            pltpu.SemaphoreType.DMA((1 + WIDTH // CHUNK,)),
        ],
        compiler_params=pltpu.CompilerParams(vmem_limit_bytes=24 * 1024 * 1024),
        cost_estimate=pl.CostEstimate(flops=806_000_000, bytes_accessed=3_500_000, transcendentals=0),
        name="pairs",
    )(scale, offset, images, texts)
    sums = exchange(term, ("z",))

    pieces = N_PLANE // 2
    kept, sent = call(
        image_terms_body, [((pieces, PIECE, LANES), F32), ((pieces, PIECE, LANES), BF)],
        (scale, images, texts, weight), [VMEM] * 4, "image_terms",
        flops=403_000_000, moved=4_700_000,
    )
    own, one, two, three = call(
        add_core_body, [((4, PIECE, LANES), F32)] + [((4, PIECE, LANES), BF)] * 3,
        (kept, other_core(sent)), [VMEM, VMEM], "add_core", moved=3_000_000,
    )
    mine, one, two, three = call(
        add_x_body, [((PIECE, LANES), F32)] + [((PIECE, LANES), BF)] * 3,
        (own, along_x(two, 2), along_x(three, 3), along_x(one, 1)),
        [VMEM] * 4, "add_x", moved=1_200_000,
    )
    (image_grad,) = call(
        add_y_body, [((BLOCK, COLUMNS), F32)],
        (mine, along_y(two, 2), along_y(one, 1), along_y(three, 3)),
        [VMEM] * 4, "add_y", moved=350_000,
    )

    text_grad, loss = call(
        text_body, [((SHARD, WIDTH), F32), ((N_PLANE, 8, LANES), F32)], (sums, u_txt, inv_txt, image_grad),
        [VMEM] * 3 + [pl.BlockSpec(memory_space=pl.ANY)], "text", moved=1_000_000,
    )
    loss = exchange(loss, PLANE)
    loss = jnp.sum(loss[:, 0, 0]).reshape(1) * (1.0 / PAIRS)
    return loss, image_grad, text_grad


def solution(mesh):
    parts = Mesh(mesh.devices.reshape(PARTS), NAMES)
    return jax.shard_map(
        on_device,
        mesh=parts,
        in_specs=(P(DP, MP), P(DP, MP), P(MP, None), P(MP, None), P(), P()),
        out_specs=(P(), P(DP, MP), P(DP + MP, None)),
        check_vma=False,
    )
```

```python
import jax
import jax.numpy as jnp
from jax import lax
from jax.experimental import pallas as pl
from jax.experimental.pallas import tpu as pltpu
from jax.sharding import Mesh, PartitionSpec as P

EPSILON = 1e-06
BF = jnp.bfloat16
F32 = jnp.float32

PARTS = (2, 16, 2, 2, 4)
NAMES = ("xh", "z", "core", "xl", "y")
DP = ("xh", "z", "core")
MP = ("xl", "y")
X = ("xh", "xl")
PLANE = ("xh", "core", "xl", "y")
N_MP = 8
N_PLANE = 32
N_Z = 16
PAIRS = 8192
SHARD = 16
WIDTH = 1536
COLUMNS = WIDTH // N_MP
BLOCK = 128
IMAGES = N_PLANE * SHARD
TEXTS = N_Z * SHARD
LANES = 128
WIDE = WIDTH + LANES
HALF = BLOCK // 2
PIECE = BLOCK + HALF

CHUNK = 512
COPIED = 4
VMEM = pl.BlockSpec(memory_space=pltpu.VMEM)
HBM = pl.BlockSpec(memory_space=pltpu.HBM)


def exchange(value, axes):
    return lax.all_to_all(value, axes, 0, 0, tiled=True)


def other_core(value):
    return lax.ppermute(value, "core", [(0, 1), (1, 0)])


def along_x(value, flip):
    return lax.ppermute(value, X, [(i, i ^ flip) for i in range(4)])


def along_y(value, step):
    return lax.ppermute(value, "y", [(i, (i + step) % 4) for i in range(4)])


def call(body, outs, operands, specs, name, flops=0, moved=0):
    return pl.pallas_call(
        body,
        out_shape=[jax.ShapeDtypeStruct(shape, dtype) for shape, dtype in outs],
        in_specs=specs,
        out_specs=[VMEM] * len(outs),
        compiler_params=pltpu.CompilerParams(vmem_limit_bytes=24 * 1024 * 1024),
        cost_estimate=pl.CostEstimate(flops=flops, bytes_accessed=moved, transcendentals=0),
        name=name,
    )(*operands)


def dot(a, b, contract):
    return lax.dot_general(a, b, (contract, ((), ())), preferred_element_type=F32)


def terms(similarity, scale, offset, labels):
    value = -labels * (scale * similarity + offset)
    small = jnp.exp(-jnp.abs(value))
    loss = jnp.maximum(value, 0.0) + jnp.log1p(small)
    share = 1.0 / (1.0 + small)
    sigmoid = jnp.where(value >= 0.0, share, small * share)
    return loss, (-labels * sigmoid).astype(BF)


def loss_tag(total, rows):
    loss = jnp.broadcast_to(total, (rows, LANES))
    high = loss.astype(BF)
    low = (loss - high.astype(F32)).astype(BF)
    lane = lax.broadcasted_iota(jnp.int32, (rows, LANES), 1)
    tag = jnp.where(lane == 0, high.astype(F32), jnp.where(lane == 1, low.astype(F32), 0.0))
    return tag.astype(BF)


def normalize_body(parts_ref, images_hbm, text_ref, u_ref, inverse_ref, images_ref, sems):
    copies = []
    for at in (0, SHARD):
        rows = slice(at, at + SHARD)
        u = parts_ref[0, rows].astype(F32)
        for member in range(1, N_MP):
            u = u + parts_ref[member, rows].astype(F32)
        inverse = lax.rsqrt(jnp.sum(u * u, axis=1, keepdims=True) + EPSILON)
        unit = (u * inverse).astype(BF)
        if at:
            text_ref[...] = unit
            u_ref[...] = u
            inverse_ref[...] = jnp.broadcast_to(inverse, inverse_ref.shape)
        else:
            tag = loss_tag(inverse, SHARD)
            for piece in range(COPIED):
                images_ref[piece, :, :WIDTH] = unit
                images_ref[piece, :, WIDTH:] = tag
            for start in range(0, N_PLANE, COPIED):
                target = images_hbm.at[pl.ds(start, COPIED)]
                copies.append(pltpu.make_async_copy(images_ref, target, sems.at[start // COPIED]))
                copies[-1].start()
    for copy in copies:
        copy.wait()


def pairs_body(scale_ref, offset_ref, images_ref, texts_ref, weight_hbm, out_hbm, weight_ref, sums_ref, sems):
    scale, offset = scale_ref[...], offset_ref[...]
    at_plane, at_z = lax.axis_index(PLANE), lax.axis_index("z")
    copies = []

    def send(source, target):
        copies.append(pltpu.make_async_copy(source, target, sems.at[len(copies)]))
        copies[-1].start()

    total = jnp.zeros((1, TEXTS), F32)
    for block in range(IMAGES // BLOCK):
        rows = pl.ds(block * BLOCK, BLOCK)
        similarity = dot(images_ref[rows, :WIDTH], texts_ref[...], ((1,), (1,)))
        image = lax.broadcasted_iota(jnp.int32, similarity.shape, 0) + block * BLOCK
        text = lax.broadcasted_iota(jnp.int32, similarity.shape, 1)
        same = (image // SHARD == at_plane) & (image - SHARD * at_plane == text - SHARD * at_z)
        loss, weight = terms(similarity, scale, offset, jnp.where(same, 1.0, -1.0))
        total = total + jnp.sum(loss, axis=0, keepdims=True)
        weight_ref[rows, :] = weight
    send(weight_ref, weight_hbm)
    tag = loss_tag(jnp.sum(total, axis=1, keepdims=True), SHARD)
    for plane in range(N_Z):
        sums_ref[plane, :, WIDTH:] = tag
    for start in range(0, WIDTH, CHUNK):
        cols = pl.ds(start, CHUNK)
        grad = scale * dot(weight_ref[...], images_ref[:, cols], ((0,), (0,)))
        for plane in range(N_Z):
            sums_ref[plane, :, cols] = grad[plane * SHARD : (plane + 1) * SHARD].astype(BF)
        cols = pl.ds(start, CHUNK + (LANES if start + CHUNK == WIDTH else 0))
        send(sums_ref.at[:, :, cols], out_hbm.at[:, :, cols])
    for copy in copies:
        copy.wait()


def image_terms_body(scale_ref, images_ref, texts_ref, weight_ref, kept_ref, sent_ref):
    scale = scale_ref[...]
    core = lax.axis_index("core")
    for hi in range(2):
        for side_ref, side in ((sent_ref, 1 - core), (kept_ref, core)):
            rows = pl.ds(pl.multiple_of((hi * 2 + side) * BLOCK, BLOCK), BLOCK)
            grad = dot(weight_ref[rows, :], texts_ref[...], ((1,), (0,)))
            images = images_ref[rows, :WIDTH].astype(F32)
            radial = jnp.sum(images * grad, axis=1, keepdims=True)
            tags = images_ref[rows, WIDTH:].astype(F32)
            inverse = tags[:, 0:1] + tags[:, 1:2]
            term = (grad - images * radial) * (scale * inverse)
            for part in range(N_MP):
                at = part * COLUMNS
                piece = hi * N_MP + part
                side_ref[piece, :BLOCK] = term[:, at : at + BLOCK].astype(side_ref.dtype)
                rest = term[:, at + BLOCK : at + COLUMNS]
                rest = jnp.concatenate([rest[:HALF], rest[HALF:]], axis=1)
                side_ref[piece, BLOCK:] = rest.astype(side_ref.dtype)


def add_core_body(kept_ref, other_ref, own_ref, one_ref, two_ref, three_ref):
    at_x = lax.axis_index(X)
    for flip, out_ref in enumerate((own_ref, one_ref, two_ref, three_ref)):
        first = jnp.bitwise_xor(at_x, flip) * 4
        for y in range(4):
            total = kept_ref[first + y] + other_ref[first + y].astype(F32)
            out_ref[y] = total.astype(out_ref.dtype)


def add_x_body(own_ref, a_ref, b_ref, c_ref, mine_ref, one_ref, two_ref, three_ref):
    at_y = lax.axis_index("y")
    for step, out_ref in enumerate((mine_ref, one_ref, two_ref, three_ref)):
        y = lax.rem(at_y + step, 4)
        total = own_ref[y] + a_ref[y].astype(F32) + (b_ref[y].astype(F32) + c_ref[y].astype(F32))
        out_ref[...] = total.astype(out_ref.dtype)


def add_y_body(mine_ref, a_ref, b_ref, c_ref, grad_ref):
    total = mine_ref[...] + a_ref[...].astype(F32)
    total = total + (b_ref[...].astype(F32) + c_ref[...].astype(F32))
    grad_ref[:, :LANES] = total[:BLOCK]
    grad_ref[:HALF, LANES:] = total[BLOCK:, :HALF]
    grad_ref[HALF:, LANES:] = total[BLOCK:, HALF:]


def text_body(sums_ref, u_ref, inverse_ref, image_ref, grad_ref, loss_ref):
    total = sums_ref[0].astype(F32)
    for block in range(1, N_Z):
        total = total + sums_ref[block].astype(F32)
    tags = total[0:1, WIDTH:]
    loss_ref[...] = jnp.broadcast_to((tags[:, 0:1] + tags[:, 1:2])[None], loss_ref.shape)
    grad = total[:, :WIDTH]
    u = u_ref[...]
    inverse = inverse_ref[:, 0:1]
    row_dot = jnp.sum(u * grad, axis=1, keepdims=True)
    grad_ref[...] = inverse * grad - inverse * inverse * inverse * u * row_dot


def on_device(x_img, x_txt, w_img, w_txt, sharpness_factor, offset_vector):
    part_img = jnp.dot(x_img, w_img, preferred_element_type=F32).astype(BF)
    part_txt = jnp.dot(x_txt, w_txt, preferred_element_type=F32).astype(BF)
    parts = jnp.concatenate(
        [part_img.reshape(N_MP, SHARD, WIDTH), part_txt.reshape(N_MP, SHARD, WIDTH)], axis=1
    )
    parts = exchange(parts, MP)
    unit_img, unit_txt, u_txt, inv_txt = pl.pallas_call(
        normalize_body,
        out_shape=[
            pltpu.HBM((N_PLANE, SHARD, WIDE), BF),
            jax.ShapeDtypeStruct((SHARD, WIDTH), BF),
            jax.ShapeDtypeStruct((SHARD, WIDTH), F32),
            jax.ShapeDtypeStruct((SHARD, LANES), F32),
        ],
        in_specs=[VMEM],
        out_specs=[HBM, VMEM, VMEM, VMEM],
        scratch_shapes=[
            pltpu.VMEM((COPIED, SHARD, WIDE), BF),
            pltpu.SemaphoreType.DMA((N_PLANE // COPIED,)),
        ],
        compiler_params=pltpu.CompilerParams(vmem_limit_bytes=24 * 1024 * 1024),
        cost_estimate=pl.CostEstimate(flops=0, bytes_accessed=2_700_000, transcendentals=0),
        name="normalize",
    )(parts)

    images = exchange(unit_img, PLANE)
    images = images.reshape(IMAGES, WIDE)
    texts = lax.all_gather(unit_txt, ("z",), axis=0, tiled=True)

    scale, offset = sharpness_factor.reshape(1, 1), offset_vector.reshape(1, 1)
    weight, term = pl.pallas_call(
        pairs_body,
        out_shape=[pltpu.HBM((IMAGES, TEXTS), BF), pltpu.HBM((N_Z, SHARD, WIDE), BF)],
        in_specs=[VMEM] * 4,
        out_specs=[HBM, HBM],
        scratch_shapes=[
            pltpu.VMEM((IMAGES, TEXTS), BF),
            pltpu.VMEM((N_Z, SHARD, WIDE), BF),
            pltpu.SemaphoreType.DMA((1 + WIDTH // CHUNK,)),
        ],
        compiler_params=pltpu.CompilerParams(vmem_limit_bytes=24 * 1024 * 1024),
        cost_estimate=pl.CostEstimate(flops=806_000_000, bytes_accessed=3_500_000, transcendentals=0),
        name="pairs",
    )(scale, offset, images, texts)
    sums = exchange(term, ("z",))

    pieces = N_PLANE // 2
    kept, sent = call(
        image_terms_body, [((pieces, PIECE, LANES), F32), ((pieces, PIECE, LANES), BF)],
        (scale, images, texts, weight), [VMEM] * 4, "image_terms",
        flops=403_000_000, moved=4_700_000,
    )
    own, one, two, three = call(
        add_core_body, [((4, PIECE, LANES), F32)] + [((4, PIECE, LANES), BF)] * 3,
        (kept, other_core(sent)), [VMEM, VMEM], "add_core", moved=3_000_000,
    )
    mine, one, two, three = call(
        add_x_body, [((PIECE, LANES), F32)] + [((PIECE, LANES), BF)] * 3,
        (own, along_x(two, 2), along_x(one, 1), along_x(three, 3)),
        [VMEM] * 4, "add_x", moved=1_200_000,
    )
    (image_grad,) = call(
        add_y_body, [((BLOCK, COLUMNS), F32)],
        (mine, along_y(two, 2), along_y(three, 3), along_y(one, 1)),
        [VMEM] * 4, "add_y", moved=350_000,
    )

    text_grad, loss = call(
        text_body, [((SHARD, WIDTH), F32), ((N_PLANE, 1, LANES), F32)], (sums, u_txt, inv_txt, image_grad),
        [VMEM] * 3 + [pl.BlockSpec(memory_space=pl.ANY)], "text", moved=1_000_000,
    )
    loss = exchange(loss, PLANE)
    loss = jnp.sum(loss[:, 0, 0]).reshape(1) * (1.0 / PAIRS)
    return loss, image_grad, text_grad


def solution(mesh):
    parts = Mesh(mesh.devices.reshape(PARTS), NAMES)
    return jax.shard_map(
        on_device,
        mesh=parts,
        in_specs=(P(DP, MP), P(DP, MP), P(MP, None), P(MP, None), P(), P()),
        out_specs=(P(), P(DP, MP), P(DP + MP, None)),
        check_vma=False,
    )
```

```python
import jax
import jax.numpy as jnp
from jax import lax
from jax.experimental import pallas as pl
from jax.experimental.pallas import tpu as pltpu
from jax.sharding import Mesh, PartitionSpec as P

EPSILON = 1e-06
BF = jnp.bfloat16
F32 = jnp.float32

PARTS = (2, 16, 2, 2, 4)
NAMES = ("xh", "z", "core", "xl", "y")
DP = ("xh", "z", "core")
MP = ("xl", "y")
X = ("xh", "xl")
PLANE = ("xh", "core", "xl", "y")
N_MP = 8
N_PLANE = 32
N_Z = 16
PAIRS = 8192
SHARD = 16
WIDTH = 1536
COLUMNS = WIDTH // N_MP
BLOCK = 128
IMAGES = N_PLANE * SHARD
TEXTS = N_Z * SHARD
LANES = 128
WIDE = WIDTH + LANES
TEXT_ROWS = WIDTH // LANES * SHARD
HALF = BLOCK // 2
PIECE = BLOCK + HALF

CHUNK = 512
COPIED = 4
VMEM = pl.BlockSpec(memory_space=pltpu.VMEM)
HBM = pl.BlockSpec(memory_space=pltpu.HBM)


def exchange(value, axes):
    return lax.all_to_all(value, axes, 0, 0, tiled=True)


def other_core(value):
    return lax.ppermute(value, "core", [(0, 1), (1, 0)])


def along_x(value, flip):
    return lax.ppermute(value, X, [(i, i ^ flip) for i in range(4)])


def along_y(value, step):
    return lax.ppermute(value, "y", [(i, (i + step) % 4) for i in range(4)])


def call(body, outs, operands, specs, name, flops=0, moved=0):
    return pl.pallas_call(
        body,
        out_shape=[jax.ShapeDtypeStruct(shape, dtype) for shape, dtype in outs],
        in_specs=specs,
        out_specs=[VMEM] * len(outs),
        compiler_params=pltpu.CompilerParams(vmem_limit_bytes=24 * 1024 * 1024),
        cost_estimate=pl.CostEstimate(flops=flops, bytes_accessed=moved, transcendentals=0),
        name=name,
    )(*operands)


def dot(a, b, contract):
    return lax.dot_general(a, b, (contract, ((), ())), preferred_element_type=F32)


def terms(similarity, scale, offset, labels):
    value = -labels * (scale * similarity + offset)
    small = jnp.exp(-jnp.abs(value))
    loss = jnp.maximum(value, 0.0) + jnp.log1p(small)
    share = 1.0 / (1.0 + small)
    sigmoid = jnp.where(value >= 0.0, share, small * share)
    return loss, (-labels * sigmoid).astype(BF)


def loss_tag(total, rows):
    loss = jnp.broadcast_to(total, (rows, LANES))
    high = loss.astype(BF)
    low = (loss - high.astype(F32)).astype(BF)
    lane = lax.broadcasted_iota(jnp.int32, (rows, LANES), 1)
    tag = jnp.where(lane == 0, high.astype(F32), jnp.where(lane == 1, low.astype(F32), 0.0))
    return tag.astype(BF)


def normalize_body(parts_ref, images_hbm, text_ref, u_ref, inverse_ref, images_ref, sems):
    copies = []
    for at in (0, SHARD):
        rows = slice(at, at + SHARD)
        u = parts_ref[0, rows].astype(F32)
        for member in range(1, N_MP):
            u = u + parts_ref[member, rows].astype(F32)
        inverse = lax.rsqrt(jnp.sum(u * u, axis=1, keepdims=True) + EPSILON)
        unit = (u * inverse).astype(BF)
        if at:
            text_ref[...] = unit
            u_ref[...] = u
            inverse_ref[...] = jnp.broadcast_to(inverse, inverse_ref.shape)
        else:
            tag = loss_tag(inverse, SHARD)
            for piece in range(COPIED):
                images_ref[piece, :, :WIDTH] = unit
                images_ref[piece, :, WIDTH:] = tag
            for start in range(0, N_PLANE, COPIED):
                target = images_hbm.at[pl.ds(start, COPIED)]
                copies.append(pltpu.make_async_copy(images_ref, target, sems.at[start // COPIED]))
                copies[-1].start()
    for copy in copies:
        copy.wait()


def pairs_body(scale_ref, offset_ref, images_ref, texts_ref, weight_hbm, out_hbm, weight_ref, sums_ref, sems):
    scale, offset = scale_ref[...], offset_ref[...]
    at_plane, at_z = lax.axis_index(PLANE), lax.axis_index("z")
    copies = []

    def send(source, target):
        copies.append(pltpu.make_async_copy(source, target, sems.at[len(copies)]))
        copies[-1].start()

    total = jnp.zeros((1, TEXTS), F32)
    for block in range(IMAGES // BLOCK):
        rows = pl.ds(block * BLOCK, BLOCK)
        similarity = dot(images_ref[rows, :WIDTH], texts_ref[...], ((1,), (1,)))
        image = lax.broadcasted_iota(jnp.int32, similarity.shape, 0) + block * BLOCK
        text = lax.broadcasted_iota(jnp.int32, similarity.shape, 1)
        same = (image // SHARD == at_plane) & (image - SHARD * at_plane == text - SHARD * at_z)
        loss, weight = terms(similarity, scale, offset, jnp.where(same, 1.0, -1.0))
        total = total + jnp.sum(loss, axis=0, keepdims=True)
        weight_ref[rows, :] = weight
    send(weight_ref, weight_hbm)
    tag = loss_tag(jnp.sum(total, axis=1, keepdims=True), SHARD)
    for plane in range(N_Z):
        sums_ref[plane, TEXT_ROWS:] = tag
    for start in range(0, WIDTH, CHUNK):
        cols = pl.ds(start, CHUNK)
        grad = scale * dot(weight_ref[...], images_ref[:, cols], ((0,), (0,)))
        for plane in range(N_Z):
            for part in range(CHUNK // LANES):
                piece = grad[plane * SHARD : (plane + 1) * SHARD, part * LANES : (part + 1) * LANES]
                row = (start // LANES + part) * SHARD
                sums_ref[plane, row : row + SHARD] = piece.astype(BF)
        first = start // LANES * SHARD
        size = CHUNK // LANES * SHARD + (8 if start + CHUNK == WIDTH else 0)
        some = pl.ds(first, size)
        send(sums_ref.at[:, some], out_hbm.at[:, some])
    for copy in copies:
        copy.wait()


def image_terms_body(scale_ref, images_ref, texts_ref, weight_ref, kept_ref, sent_ref):
    scale = scale_ref[...]
    core = lax.axis_index("core")
    for hi in range(2):
        for side_ref, side in ((sent_ref, 1 - core), (kept_ref, core)):
            rows = pl.ds(pl.multiple_of((hi * 2 + side) * BLOCK, BLOCK), BLOCK)
            grad = dot(weight_ref[rows, :], texts_ref[...], ((1,), (0,)))
            images = images_ref[rows, :WIDTH].astype(F32)
            radial = jnp.sum(images * grad, axis=1, keepdims=True)
            tags = images_ref[rows, WIDTH:].astype(F32)
            inverse = tags[:, 0:1] + tags[:, 1:2]
            term = (grad - images * radial) * (scale * inverse)
            for part in range(N_MP):
                at = part * COLUMNS
                piece = hi * N_MP + part
                side_ref[piece, :BLOCK] = term[:, at : at + BLOCK].astype(side_ref.dtype)
                rest = term[:, at + BLOCK : at + COLUMNS]
                rest = jnp.concatenate([rest[:HALF], rest[HALF:]], axis=1)
                side_ref[piece, BLOCK:] = rest.astype(side_ref.dtype)


def add_core_body(kept_ref, other_ref, own_ref, one_ref, two_ref, three_ref):
    at_x = lax.axis_index(X)
    for flip, out_ref in enumerate((own_ref, one_ref, two_ref, three_ref)):
        first = jnp.bitwise_xor(at_x, flip) * 4
        for y in range(4):
            total = kept_ref[first + y] + other_ref[first + y].astype(F32)
            out_ref[y] = total.astype(out_ref.dtype)


def add_x_body(own_ref, a_ref, b_ref, c_ref, mine_ref, one_ref, two_ref, three_ref):
    at_y = lax.axis_index("y")
    for step, out_ref in enumerate((mine_ref, one_ref, two_ref, three_ref)):
        y = lax.rem(at_y + step, 4)
        total = own_ref[y] + a_ref[y].astype(F32) + (b_ref[y].astype(F32) + c_ref[y].astype(F32))
        out_ref[...] = total.astype(out_ref.dtype)


def add_two_body(mine_ref, a_ref, b_ref, sum_ref):
    sum_ref[...] = mine_ref[...] + (a_ref[...].astype(F32) + b_ref[...].astype(F32))


def add_last_body(sum_ref, a_ref, grad_ref):
    total = sum_ref[...] + a_ref[...].astype(F32)
    grad_ref[:, :LANES] = total[:BLOCK]
    grad_ref[:HALF, LANES:] = total[BLOCK:, :HALF]
    grad_ref[HALF:, LANES:] = total[BLOCK:, HALF:]


def text_body(sums_ref, u_ref, inverse_ref, image_ref, grad_ref, loss_ref):
    total = sums_ref[0].astype(F32)
    for block in range(1, N_Z):
        total = total + sums_ref[block].astype(F32)
    tags = total[TEXT_ROWS : TEXT_ROWS + 1]
    loss_ref[...] = jnp.broadcast_to((tags[:, 0:1] + tags[:, 1:2])[None], loss_ref.shape)
    grad = jnp.concatenate([total[row : row + SHARD] for row in range(0, TEXT_ROWS, SHARD)], axis=1)
    u = u_ref[...]
    inverse = inverse_ref[:, 0:1]
    row_dot = jnp.sum(u * grad, axis=1, keepdims=True)
    grad_ref[...] = inverse * grad - inverse * inverse * inverse * u * row_dot


def on_device(x_img, x_txt, w_img, w_txt, sharpness_factor, offset_vector):
    part_img = jnp.dot(x_img, w_img, preferred_element_type=F32).astype(BF)
    part_txt = jnp.dot(x_txt, w_txt, preferred_element_type=F32).astype(BF)
    parts = jnp.concatenate(
        [part_img.reshape(N_MP, SHARD, WIDTH), part_txt.reshape(N_MP, SHARD, WIDTH)], axis=1
    )
    parts = exchange(parts, MP)
    unit_img, unit_txt, u_txt, inv_txt = pl.pallas_call(
        normalize_body,
        out_shape=[
            pltpu.HBM((N_PLANE, SHARD, WIDE), BF),
            jax.ShapeDtypeStruct((SHARD, WIDTH), BF),
            jax.ShapeDtypeStruct((SHARD, WIDTH), F32),
            jax.ShapeDtypeStruct((SHARD, LANES), F32),
        ],
        in_specs=[VMEM],
        out_specs=[HBM, VMEM, VMEM, VMEM],
        scratch_shapes=[
            pltpu.VMEM((COPIED, SHARD, WIDE), BF),
            pltpu.SemaphoreType.DMA((N_PLANE // COPIED,)),
        ],
        compiler_params=pltpu.CompilerParams(vmem_limit_bytes=24 * 1024 * 1024),
        cost_estimate=pl.CostEstimate(flops=0, bytes_accessed=2_700_000, transcendentals=0),
        name="normalize",
    )(parts)

    images = exchange(unit_img, PLANE)
    images = images.reshape(IMAGES, WIDE)
    texts = lax.all_gather(unit_txt, ("z",), axis=0, tiled=True)

    scale, offset = sharpness_factor.reshape(1, 1), offset_vector.reshape(1, 1)
    weight, term = pl.pallas_call(
        pairs_body,
        out_shape=[pltpu.HBM((IMAGES, TEXTS), BF), pltpu.HBM((N_Z, TEXT_ROWS + 8, LANES), BF)],
        in_specs=[VMEM] * 4,
        out_specs=[HBM, HBM],
        scratch_shapes=[
            pltpu.VMEM((IMAGES, TEXTS), BF),
            pltpu.VMEM((N_Z, TEXT_ROWS + SHARD, LANES), BF),
            pltpu.SemaphoreType.DMA((1 + WIDTH // CHUNK,)),
        ],
        compiler_params=pltpu.CompilerParams(vmem_limit_bytes=24 * 1024 * 1024),
        cost_estimate=pl.CostEstimate(flops=806_000_000, bytes_accessed=3_500_000, transcendentals=0),
        name="pairs",
    )(scale, offset, images, texts)
    sums = exchange(term, ("z",))

    pieces = N_PLANE // 2
    kept, sent = call(
        image_terms_body, [((pieces, PIECE, LANES), F32), ((pieces, PIECE, LANES), BF)],
        (scale, images, texts, weight), [VMEM] * 4, "image_terms",
        flops=403_000_000, moved=4_700_000,
    )
    own, one, two, three = call(
        add_core_body, [((4, PIECE, LANES), F32)] + [((4, PIECE, LANES), BF)] * 3,
        (kept, other_core(sent)), [VMEM, VMEM], "add_core", moved=3_000_000,
    )
    mine, one, two, three = call(
        add_x_body, [((PIECE, LANES), F32)] + [((PIECE, LANES), BF)] * 3,
        (own, along_x(two, 2), along_x(one, 1), along_x(three, 3)),
        [VMEM] * 4, "add_x", moved=1_200_000,
    )
    last = along_y(two, 2)
    (total,) = call(
        add_two_body, [((PIECE, LANES), F32)], (mine, along_y(one, 1), along_y(three, 3)),
        [VMEM] * 3, "add_two", moved=250_000,
    )
    (image_grad,) = call(
        add_last_body, [((BLOCK, COLUMNS), F32)], (total, last), [VMEM] * 2, "add_last", moved=250_000,
    )

    text_grad, loss = call(
        text_body, [((SHARD, WIDTH), F32), ((N_PLANE, 1, LANES), F32)], (sums, u_txt, inv_txt, total),
        [VMEM] * 3 + [pl.BlockSpec(memory_space=pl.ANY)], "text", moved=1_000_000,
    )
    loss = exchange(loss, PLANE)
    loss = jnp.sum(loss[:, 0, 0]).reshape(1) * (1.0 / PAIRS)
    return loss, image_grad, text_grad


def solution(mesh):
    parts = Mesh(mesh.devices.reshape(PARTS), NAMES)
    return jax.shard_map(
        on_device,
        mesh=parts,
        in_specs=(P(DP, MP), P(DP, MP), P(MP, None), P(MP, None), P(), P()),
        out_specs=(P(), P(DP, MP), P(DP + MP, None)),
        check_vma=False,
    )
```

```python
import jax
import jax.numpy as jnp
from jax import lax
from jax.experimental import pallas as pl
from jax.experimental.pallas import tpu as pltpu
from jax.sharding import Mesh, PartitionSpec as P

EPSILON = 1e-06
BF = jnp.bfloat16
F32 = jnp.float32

PARTS = (2, 16, 2, 2, 4)
NAMES = ("xh", "z", "core", "xl", "y")
DP = ("xh", "z", "core")
MP = ("xl", "y")
X = ("xh", "xl")
PLANE = ("xh", "core", "xl", "y")
N_MP = 8
N_PLANE = 32
N_Z = 16
PAIRS = 8192
SHARD = 16
WIDTH = 1536
COLUMNS = WIDTH // N_MP
BLOCK = 128
IMAGES = N_PLANE * SHARD
TEXTS = N_Z * SHARD
LANES = 128
WIDE = WIDTH + LANES
HALF = BLOCK // 2
PIECE = BLOCK + HALF

CHUNK = 512
COPIED = 4
VMEM = pl.BlockSpec(memory_space=pltpu.VMEM)
HBM = pl.BlockSpec(memory_space=pltpu.HBM)


def exchange(value, axes):
    return lax.all_to_all(value, axes, 0, 0, tiled=True)


def other_core(value):
    return lax.ppermute(value, "core", [(0, 1), (1, 0)])


def along_x(value, flip):
    return lax.ppermute(value, X, [(i, i ^ flip) for i in range(4)])


def along_y(value, step):
    return lax.ppermute(value, "y", [(i, (i + step) % 4) for i in range(4)])


def call(body, outs, operands, specs, name, flops=0, moved=0):
    return pl.pallas_call(
        body,
        out_shape=[jax.ShapeDtypeStruct(shape, dtype) for shape, dtype in outs],
        in_specs=specs,
        out_specs=[VMEM] * len(outs),
        compiler_params=pltpu.CompilerParams(vmem_limit_bytes=24 * 1024 * 1024),
        cost_estimate=pl.CostEstimate(flops=flops, bytes_accessed=moved, transcendentals=0),
        name=name,
    )(*operands)


def dot(a, b, contract):
    return lax.dot_general(a, b, (contract, ((), ())), preferred_element_type=F32)


def weigh(similarity, scale, offset, labels):
    value = -labels * (scale * similarity + offset)
    small = jnp.exp(-jnp.abs(value))
    share = 1.0 / (1.0 + small)
    sigmoid = jnp.where(value >= 0.0, share, small * share)
    return value, (-labels * sigmoid).astype(BF)


def softplus(value):
    return jnp.maximum(value, 0.0) + jnp.log1p(jnp.exp(-jnp.abs(value)))


def loss_tag(total, rows):
    loss = jnp.broadcast_to(total, (rows, LANES))
    high = loss.astype(BF)
    low = (loss - high.astype(F32)).astype(BF)
    lane = lax.broadcasted_iota(jnp.int32, (rows, LANES), 1)
    tag = jnp.where(lane == 0, high.astype(F32), jnp.where(lane == 1, low.astype(F32), 0.0))
    return tag.astype(BF)


def normalize_body(parts_ref, images_hbm, text_ref, u_ref, inverse_ref, images_ref, sems):
    copies = []
    for at in (0, SHARD):
        rows = slice(at, at + SHARD)
        u = parts_ref[0, rows].astype(F32)
        for member in range(1, N_MP):
            u = u + parts_ref[member, rows].astype(F32)
        inverse = lax.rsqrt(jnp.sum(u * u, axis=1, keepdims=True) + EPSILON)
        unit = (u * inverse).astype(BF)
        if at:
            text_ref[...] = unit
            u_ref[...] = u
            inverse_ref[...] = jnp.broadcast_to(inverse, inverse_ref.shape)
        else:
            tag = loss_tag(inverse, SHARD)
            for piece in range(COPIED):
                images_ref[piece, :, :WIDTH] = unit
                images_ref[piece, :, WIDTH:] = tag
            for start in range(0, N_PLANE, COPIED):
                target = images_hbm.at[pl.ds(start, COPIED)]
                copies.append(pltpu.make_async_copy(images_ref, target, sems.at[start // COPIED]))
                copies[-1].start()
    for copy in copies:
        copy.wait()


def pairs_body(
    scale_ref, offset_ref, images_ref, texts_ref, weight_hbm, out_hbm, weight_ref, value_ref, sums_ref, sems
):
    scale, offset = scale_ref[...], offset_ref[...]
    at_plane, at_z = lax.axis_index(PLANE), lax.axis_index("z")
    copies = []

    def send(source, target):
        copies.append(pltpu.make_async_copy(source, target, sems.at[len(copies)]))
        copies[-1].start()

    for block in range(IMAGES // BLOCK):
        rows = pl.ds(block * BLOCK, BLOCK)
        similarity = dot(images_ref[rows, :WIDTH], texts_ref[...], ((1,), (1,)))
        image = lax.broadcasted_iota(jnp.int32, similarity.shape, 0) + block * BLOCK
        text = lax.broadcasted_iota(jnp.int32, similarity.shape, 1)
        same = (image // SHARD == at_plane) & (image - SHARD * at_plane == text - SHARD * at_z)
        value, weight = weigh(similarity, scale, offset, jnp.where(same, 1.0, -1.0))
        value_ref[rows, :] = value
        weight_ref[rows, :] = weight
    for start in range(0, WIDTH, CHUNK):
        cols = pl.ds(start, CHUNK)
        grad = scale * dot(weight_ref[...], images_ref[:, cols], ((0,), (0,)))
        for plane in range(N_Z):
            sums_ref[plane, :, cols] = grad[plane * SHARD : (plane + 1) * SHARD].astype(BF)
        send(sums_ref.at[:, :, cols], out_hbm.at[:, :, cols])
    send(weight_ref, weight_hbm)
    total = jnp.zeros((1, TEXTS), F32)
    for block in range(IMAGES // BLOCK):
        rows = pl.ds(block * BLOCK, BLOCK)
        total = total + jnp.sum(softplus(value_ref[rows, :]), axis=0, keepdims=True)
    tag = loss_tag(jnp.sum(total, axis=1, keepdims=True), SHARD)
    for plane in range(N_Z):
        sums_ref[plane, :, WIDTH:] = tag
    send(sums_ref.at[:, :, WIDTH:], out_hbm.at[:, :, WIDTH:])
    for copy in copies:
        copy.wait()


def image_terms_body(scale_ref, images_ref, texts_ref, weight_ref, kept_ref, sent_ref):
    scale = scale_ref[...]
    core = lax.axis_index("core")
    for hi in range(2):
        for side_ref, side in ((sent_ref, 1 - core), (kept_ref, core)):
            rows = pl.ds(pl.multiple_of((hi * 2 + side) * BLOCK, BLOCK), BLOCK)
            grad = dot(weight_ref[rows, :], texts_ref[...], ((1,), (0,)))
            images = images_ref[rows, :WIDTH].astype(F32)
            radial = jnp.sum(images * grad, axis=1, keepdims=True)
            tags = images_ref[rows, WIDTH:].astype(F32)
            inverse = tags[:, 0:1] + tags[:, 1:2]
            term = (grad - images * radial) * (scale * inverse)
            for part in range(N_MP):
                at = part * COLUMNS
                piece = hi * N_MP + part
                side_ref[piece, :BLOCK] = term[:, at : at + BLOCK].astype(side_ref.dtype)
                rest = term[:, at + BLOCK : at + COLUMNS]
                rest = jnp.concatenate([rest[:HALF], rest[HALF:]], axis=1)
                side_ref[piece, BLOCK:] = rest.astype(side_ref.dtype)


def add_core_body(kept_ref, other_ref, own_ref, one_ref, two_ref, three_ref):
    at_x = lax.axis_index(X)
    for flip, out_ref in enumerate((own_ref, one_ref, two_ref, three_ref)):
        first = jnp.bitwise_xor(at_x, flip) * 4
        for y in range(4):
            total = kept_ref[first + y] + other_ref[first + y].astype(F32)
            out_ref[y] = total.astype(out_ref.dtype)


def add_x_body(own_ref, a_ref, b_ref, c_ref, mine_ref, one_ref, two_ref, three_ref):
    at_y = lax.axis_index("y")
    for step, out_ref in enumerate((mine_ref, one_ref, two_ref, three_ref)):
        y = lax.rem(at_y + step, 4)
        total = own_ref[y] + a_ref[y].astype(F32) + (b_ref[y].astype(F32) + c_ref[y].astype(F32))
        out_ref[...] = total.astype(out_ref.dtype)


def add_two_body(mine_ref, a_ref, b_ref, sum_ref):
    sum_ref[...] = mine_ref[...] + (a_ref[...].astype(F32) + b_ref[...].astype(F32))


def add_last_body(sum_ref, a_ref, grad_ref):
    total = sum_ref[...] + a_ref[...].astype(F32)
    grad_ref[:, :LANES] = total[:BLOCK]
    grad_ref[:HALF, LANES:] = total[BLOCK:, :HALF]
    grad_ref[HALF:, LANES:] = total[BLOCK:, HALF:]


def text_body(sums_ref, u_ref, inverse_ref, image_ref, grad_ref, loss_ref):
    total = sums_ref[0].astype(F32)
    for block in range(1, N_Z):
        total = total + sums_ref[block].astype(F32)
    tags = total[0:1, WIDTH:]
    loss_ref[...] = jnp.broadcast_to((tags[:, 0:1] + tags[:, 1:2])[None], loss_ref.shape)
    grad = total[:, :WIDTH]
    u = u_ref[...]
    inverse = inverse_ref[:, 0:1]
    row_dot = jnp.sum(u * grad, axis=1, keepdims=True)
    grad_ref[...] = inverse * grad - inverse * inverse * inverse * u * row_dot


def on_device(x_img, x_txt, w_img, w_txt, sharpness_factor, offset_vector):
    part_img = jnp.dot(x_img, w_img, preferred_element_type=F32).astype(BF)
    part_txt = jnp.dot(x_txt, w_txt, preferred_element_type=F32).astype(BF)
    parts = jnp.concatenate(
        [part_img.reshape(N_MP, SHARD, WIDTH), part_txt.reshape(N_MP, SHARD, WIDTH)], axis=1
    )
    parts = exchange(parts, MP)
    unit_img, unit_txt, u_txt, inv_txt = pl.pallas_call(
        normalize_body,
        out_shape=[
            pltpu.HBM((N_PLANE, SHARD, WIDE), BF),
            jax.ShapeDtypeStruct((SHARD, WIDTH), BF),
            jax.ShapeDtypeStruct((SHARD, WIDTH), F32),
            jax.ShapeDtypeStruct((SHARD, LANES), F32),
        ],
        in_specs=[VMEM],
        out_specs=[HBM, VMEM, VMEM, VMEM],
        scratch_shapes=[
            pltpu.VMEM((COPIED, SHARD, WIDE), BF),
            pltpu.SemaphoreType.DMA((N_PLANE // COPIED,)),
        ],
        compiler_params=pltpu.CompilerParams(vmem_limit_bytes=24 * 1024 * 1024),
        cost_estimate=pl.CostEstimate(flops=0, bytes_accessed=2_700_000, transcendentals=0),
        name="normalize",
    )(parts)

    images = exchange(unit_img, PLANE)
    images = images.reshape(IMAGES, WIDE)
    texts = lax.all_gather(unit_txt, ("z",), axis=0, tiled=True)

    scale, offset = sharpness_factor.reshape(1, 1), offset_vector.reshape(1, 1)
    weight, term = pl.pallas_call(
        pairs_body,
        out_shape=[pltpu.HBM((IMAGES, TEXTS), BF), pltpu.HBM((N_Z, SHARD, WIDE), BF)],
        in_specs=[VMEM] * 4,
        out_specs=[HBM, HBM],
        scratch_shapes=[
            pltpu.VMEM((IMAGES, TEXTS), BF),
            pltpu.VMEM((IMAGES, TEXTS), F32),
            pltpu.VMEM((N_Z, SHARD, WIDE), BF),
            pltpu.SemaphoreType.DMA((2 + WIDTH // CHUNK,)),
        ],
        compiler_params=pltpu.CompilerParams(vmem_limit_bytes=24 * 1024 * 1024),
        cost_estimate=pl.CostEstimate(flops=806_000_000, bytes_accessed=3_500_000, transcendentals=0),
        name="pairs",
    )(scale, offset, images, texts)
    sums = exchange(term, ("z",))

    pieces = N_PLANE // 2
    kept, sent = call(
        image_terms_body, [((pieces, PIECE, LANES), F32), ((pieces, PIECE, LANES), BF)],
        (scale, images, texts, weight), [VMEM] * 4, "image_terms",
        flops=403_000_000, moved=4_700_000,
    )
    own, one, two, three = call(
        add_core_body, [((4, PIECE, LANES), F32)] + [((4, PIECE, LANES), BF)] * 3,
        (kept, other_core(sent)), [VMEM, VMEM], "add_core", moved=3_000_000,
    )
    mine, one, two, three = call(
        add_x_body, [((PIECE, LANES), F32)] + [((PIECE, LANES), BF)] * 3,
        (own, along_x(two, 2), along_x(one, 1), along_x(three, 3)),
        [VMEM] * 4, "add_x", moved=1_200_000,
    )
    last = along_y(two, 2)
    (total,) = call(
        add_two_body, [((PIECE, LANES), F32)], (mine, along_y(one, 1), along_y(three, 3)),
        [VMEM] * 3, "add_two", moved=250_000,
    )
    (image_grad,) = call(
        add_last_body, [((BLOCK, COLUMNS), F32)], (total, last), [VMEM] * 2, "add_last", moved=250_000,
    )

    text_grad, loss = call(
        text_body, [((SHARD, WIDTH), F32), ((N_PLANE, 1, LANES), F32)], (sums, u_txt, inv_txt, total),
        [VMEM] * 3 + [pl.BlockSpec(memory_space=pl.ANY)], "text", moved=1_000_000,
    )
    loss = exchange(loss, PLANE)
    loss = jnp.sum(loss[:, 0, 0]).reshape(1) * (1.0 / PAIRS)
    return loss, image_grad, text_grad


def solution(mesh):
    parts = Mesh(mesh.devices.reshape(PARTS), NAMES)
    return jax.shard_map(
        on_device,
        mesh=parts,
        in_specs=(P(DP, MP), P(DP, MP), P(MP, None), P(MP, None), P(), P()),
        out_specs=(P(), P(DP, MP), P(DP + MP, None)),
        check_vma=False,
    )
```
